256 devices in a mesh: gx: 8 (over z), gy: 16 (over y, x_hi, core), gz: 2 (over x_lo).
Axes of the slice: x: 4 (x_hi: 2, x_lo: 2; x = x_hi * 2 + x_lo), y: 4, z: 8, core: 2. Of those that a mesh axis runs over, the one named last changes fastest.
Arguments:
- density: float32 [64, 1024, 256], P('gx', 'gy', 'gz'), may hold values from 0.5 to 2
- momentum: float32 [3, 64, 1024, 256], P(None, 'gx', 'gy', 'gz'), may hold values from -0.6 to 0.6
- column_shift: int32 [64], replicated, may hold values from 0 to 1023
- column_fraction: float32 [64], replicated, may hold values from 0 to 1
- shear_offset: int32 [1], replicated, may hold values from 0 to 1023
Outputs:
- density_next: float32 [64, 1024, 256], P('gx', 'gy', 'gz')
- momentum_next: float32 [3, 64, 1024, 256], P(None, 'gx', 'gy', 'gz')
The draws below stay inside these ranges and needn't reach their ends.
All inputs are finite; a program needn't handle non-finite values.
Results may differ from the reference program's by a relative error of at most 0.0003.
Values sent between devices are 32-bit elements; how exact they have to be, the bound alone decides.
No kernel may reach another device: no remote copies, remote signals or barrier semaphores. Data moves between devices by JAX's collectives and lax.ppermute only.
A program may use at most 128 MiB of HBM per device.

```python
import math
import jax
import jax.numpy as jnp
from jax import lax

NX = 64
NY = 1024
NZ = 256


def with_ends(entries, rng, smallest, largest):
    spot = [jax.random.randint(jax.random.fold_in(rng, axis), (), 0, length) for axis, length in enumerate(entries.shape)]
    longest = entries.shape.index(max(entries.shape))
    beside = spot[:longest] + [(spot[longest] + 1) % entries.shape[longest]] + spot[longest + 1:]
    return entries.at[tuple(spot)].set(smallest).at[tuple(beside)].set(largest)


def block_scale(rng, shape, pieces, least, largest):
    gain, own = 1.0, jax.random.fold_in(rng, 6)
    for dim, blocks in pieces:
        steps = jnp.exp(jax.random.uniform(jax.random.fold_in(own, dim), (blocks,), jnp.float32, least / len(pieces), largest / len(pieces)))
        gain = gain * jnp.repeat(steps, shape[dim] // blocks).reshape([-1 if axis == dim else 1 for axis in range(len(shape))])
    return gain


def gaussian(key, shape, width, most, cuts=(), held_as=jnp.bfloat16):
    array = width * jax.random.normal(key, shape, jnp.float32)
    if cuts:
        array = array * block_scale(key, shape, cuts, -0.22, 0.18)
    return jnp.clip(array, -most, most).astype(held_as)


def setup_inputs(seed: int = 0) -> dict:
    key_of = jax.random.split(jax.random.key(seed), 6)
    return {
        "density": jnp.clip(jnp.exp(math.log(2.0) - 1.3862944 * jax.random.uniform(key_of[0], (NX, NY, NZ), jnp.float32) ** block_scale(key_of[0], (NX, NY, NZ), ((0, 8), (1, 16), (2, 2)), -0.2, 0.2)), 0.5, 2.0),
        "momentum": gaussian(key_of[1], (3, NX, NY, NZ), 0.2, 0.6, ((1, 8), (2, 16), (3, 2)), jnp.float32),
        "column_shift": with_ends(jax.random.randint(key_of[2], (NX,), 0, NY), jax.random.fold_in(key_of[2], 1), 0, NY - 1).astype(jnp.int32),
        "column_fraction": jnp.clip(jax.random.uniform(key_of[3], (NX,), jnp.float32, 0.0, 1.0), 0.0, 1.0),
        "shear_offset": jax.random.randint(key_of[4], (1,), 0, NY).astype(jnp.int32),
    }


def minmod(first, second):
    return 0.5 * (jnp.sign(first) + jnp.sign(second)) * jnp.minimum(jnp.abs(first), jnp.abs(second))


def physical_flux(state, normal):
    speed = state[normal] / state[0]
    parts = [state[normal]]
    for comp in range(1, 4):
        term = state[comp] * speed
        if comp == normal:
            term = term + state[0]
        parts.append(term)
    return jnp.stack(parts, axis=0)


def sweep(extended, normal):
    count = extended.shape[normal]

    def take(arr, low, high):
        return lax.slice_in_dim(arr, low, high, axis=normal)

    lower = take(extended, 0, count - 2)
    middle = take(extended, 1, count - 1)
    upper = take(extended, 2, count)
    slope = minmod(middle - lower, upper - middle)
    minus = middle - 0.5 * slope
    plus = middle + 0.5 * slope
    change = 0.075 * (physical_flux(plus, normal) - physical_flux(minus, normal))
    minus = minus - change
    plus = plus - change
    inner = count - 2
    left = take(plus, 0, inner - 1)
    right = take(minus, 1, inner)
    speed_left = left[normal] / left[0]
    speed_right = right[normal] / right[0]
    slowest = jnp.minimum(jnp.minimum(speed_left - 1.0, speed_right - 1.0), 0.0)
    fastest = jnp.maximum(jnp.maximum(speed_left + 1.0, speed_right + 1.0), 0.0)
    face = (fastest * physical_flux(left, normal) - slowest * physical_flux(right, normal)
            + fastest * slowest * (right - left)) / (fastest - slowest)
    return take(face, 1, inner - 1) - take(face, 0, inner - 2)


def advance(remapped, ext_x, ext_y, ext_z, height):
    divergence = sweep(ext_x, 1) + sweep(ext_y, 2) + sweep(ext_z, 3)
    source = jnp.stack([jnp.zeros_like(remapped[0]), 2.0 * remapped[2], -0.5 * remapped[1],
                        -height * remapped[0]], axis=0)
    return remapped - 0.15 * divergence + 0.15 * source


def reference(density, momentum, column_shift, column_fraction, shear_offset):
    state = jnp.concatenate([density[None], momentum], axis=0)

    def remap_column(column, shift_cells, weight):
        return (1.0 - weight) * jnp.roll(column, shift_cells, axis=1) + weight * jnp.roll(column, shift_cells + 1, axis=1)

    remapped = jax.vmap(remap_column, in_axes=(1, 0, 0), out_axes=1)(state, column_shift, column_fraction)
    offset = shear_offset[0]
    inner_ghost = jnp.roll(remapped[:, -2:], offset, axis=2)
    outer_ghost = jnp.roll(remapped[:, :2], -offset, axis=2)
    padded = jnp.concatenate([inner_ghost, remapped, outer_ghost], axis=1)
    padded = jnp.concatenate([padded[:, :, -2:], padded, padded[:, :, :2]], axis=2)
    padded = jnp.pad(padded, ((0, 0), (0, 0), (0, 0), (2, 2)), mode="edge")
    half = NZ / 2.0
    height = (jnp.arange(NZ, dtype=jnp.int32).astype(jnp.float32) + 0.5 - half) / half
    slab_width = 4
    starts = jnp.arange(NX // slab_width, dtype=jnp.int32) * slab_width

    def slab(start):
        block = lax.dynamic_slice(padded, (jnp.int32(0), start, jnp.int32(0), jnp.int32(0)),
                                  (4, slab_width + 4, NY + 4, NZ + 4))
        centre = block[:, 2:-2, 2:-2, 2:-2]
        return advance(centre, block[:, :, 2:-2, 2:-2], block[:, 2:-2, :, 2:-2],
                       block[:, 2:-2, 2:-2, :], height)

    result = lax.map(slab, starts)
    result = jnp.moveaxis(result, 0, 1).reshape(4, NX, NY, NZ)
    return result[0], result[1:]
```

```python
import jax
import jax.numpy as jnp
import numpy as np
from jax import lax
from jax.experimental import pallas as pl
from jax.experimental.pallas import tpu as pltpu
from jax.sharding import PartitionSpec as P

CHIPS = [(0, 0), (1, 0), (2, 0), (3, 0), (3, 1), (2, 1), (1, 1), (0, 1)]
PATH = [(y * 2 + xh) * 2 + core for y, xh in CHIPS for core in (0, 1)]
CHUNKS = len(PATH)
DT = 0.15
F32 = jnp.float32


def params():
    return pltpu.CompilerParams(vmem_limit_bytes=48 * 1024 * 1024)


def vmem():
    return pl.BlockSpec(memory_space=pltpu.VMEM)


def smem():
    return pl.BlockSpec(memory_space=pltpu.SMEM)


def pack_kernel(dest, density, momentum, send):
    def one(xq, _):
        for c in range(4):
            if c == 0:
                pair = [density[xq], density[xq + 4]]
            else:
                pair = [momentum[c - 1, xq], momentum[c - 1, xq + 4]]
            turned = jnp.concatenate(pair, axis=0).T
            for k in range(CHUNKS):
                send[dest[k], c, xq] = turned[8 * k : 8 * k + 8]
        return 0

    lax.fori_loop(0, 4, one, 0)


def unpack_kernel(dest, recv, density, momentum):
    def one(xq, _):
        for c in range(4):
            levels = jnp.concatenate([recv[dest[k], c, xq] for k in range(CHUNKS)], axis=0)
            turned = levels.T
            if c == 0:
                density[xq] = turned[:64]
                density[xq + 4] = turned[64:]
            else:
                momentum[c - 1, xq] = turned[:64]
                momentum[c - 1, xq + 4] = turned[64:]
        return 0

    lax.fori_loop(0, 4, one, 0)


def lanes():
    return lax.broadcasted_iota(jnp.int32, (8, 128), 1)


def ring_roll(tile, shift, lane):
    far, near = shift // 128, shift % 128
    turned = pltpu.roll(tile, near, 1)
    return jnp.where(lane < near, pltpu.roll(turned, far + 1, 0), pltpu.roll(turned, far, 0))


def ring_next(tile, lane):
    turned = pltpu.roll(tile, 127, 1)
    return jnp.where(lane == 127, pltpu.roll(turned, 7, 0), turned)


def ring_prev(tile, lane):
    turned = pltpu.roll(tile, 1, 1)
    return jnp.where(lane == 0, pltpu.roll(turned, 1, 0), turned)


def remap_kernel(info, shifts, fractions, recv, rem, x_low, x_high, z_low, z_high):
    lane = lanes()
    first = info[0] * 8

    def remapped(tile, far, near, weight):
        turned = pltpu.roll(tile, near, 1)
        here = jnp.where(lane < near, pltpu.roll(turned, far + 1, 0), pltpu.roll(turned, far, 0))
        before = ring_prev(here, lane)
        return (1.0 - weight) * here + weight * before

    def one(c, _):
        for xq in range(4):
            cols = (xq, xq + 4)
            shift = [shifts[first + x] for x in cols]
            far = [lax.shift_right_logical(s, 7) for s in shift]
            near = [lax.bitwise_and(s, 127) for s in shift]
            weight = [fractions[first + x] for x in cols]
            for z in range(8):
                base = (c * 4 + xq) * 8 + z
                even = recv[pl.ds(base, 8, stride=256), :]
                odd = recv[pl.ds(base + 128, 8, stride=256), :]
                tiles = (
                    jnp.where(lane < 64, even, pltpu.roll(odd, 64, 1)),
                    jnp.where(lane < 64, pltpu.roll(even, 64, 1), odd),
                )
                for i, x in enumerate(cols):
                    value = remapped(tiles[i], far[i], near[i], weight[i])
                    rem[c, x, z] = value
                    if x < 2:
                        x_low[c, x, z] = value
                    if x >= 6:
                        x_high[c, x - 6, z] = value
                    if z < 2:
                        z_low[c, x, z] = value
                    if z >= 6:
                        z_high[c, x, z - 6] = value
        return 0

    lax.fori_loop(0, 4, one, 0)


def minmod(a, b):
    return jnp.maximum(jnp.minimum(a, b), 0.0) + jnp.minimum(jnp.maximum(a, b), 0.0)


def predict(cell, below, above, k):
    slope = [minmod(below[c], above[c]) for c in range(4)]
    half = [0.5 * s for s in slope]
    minus = [cell[c] - half[c] for c in range(4)]
    plus = [cell[c] + half[c] for c in range(4)]
    v_minus = minus[k] / minus[0]
    v_plus = plus[k] / plus[0]
    change = [0.075 * slope[k]]
    for c in range(1, 4):
        term = plus[c] * v_plus - minus[c] * v_minus
        if c == k:
            term = term + slope[0]
        change.append(0.075 * term)
    return [minus[c] - change[c] for c in range(4)], [plus[c] - change[c] for c in range(4)]


def face_flux(left, right, k, v_left, v_right):
    slowest = jnp.minimum(jnp.minimum(v_left, v_right) - 1.0, 0.0)
    fastest = jnp.maximum(jnp.maximum(v_left, v_right) + 1.0, 0.0)
    scale = 1.0 / (fastest - slowest)
    up = fastest * scale
    down = -slowest * scale
    mix = fastest * slowest * scale
    from_left = up * v_left - mix
    from_right = down * v_right + mix
    flux = [left[c] * from_left + right[c] * from_right for c in range(4)]
    flux[k] = flux[k] + (up * left[0] + down * right[0])
    return flux


def along_kernel(info, rem, acc):
    lane = lanes()

    def one(x, _):
        for z in range(8):
            cell = [rem[c, x, z] for c in range(4)]
            below = [u - ring_prev(u, lane) for u in cell]
            above = [ring_next(d, lane) for d in below]
            minus, plus = predict(cell, below, above, 2)
            v_minus = minus[2] / minus[0]
            v_plus = plus[2] / plus[0]
            right = [ring_next(m, lane) for m in minus]
            flux = face_flux(plus, right, 2, v_plus, ring_next(v_minus, lane))
            div = [f - ring_prev(f, lane) for f in flux]
            height = ((info[1] + z).astype(F32) + (0.5 - 128.0)) * (1.0 / 128.0)
            acc[0, x, z] = cell[0] - DT * div[0]
            acc[1, x, z] = cell[1] - DT * (div[1] - 2.0 * cell[2])
            acc[2, x, z] = cell[2] - DT * (div[2] + 0.5 * cell[1])
            acc[3, x, z] = cell[3] - DT * (div[3] + height * cell[0])
        return 0

    lax.fori_loop(0, 8, one, 0)


def march(cells, k):
    flux_before = None
    plus_before = v_before = None
    below = [b - a for a, b in zip(cells[0], cells[1])]
    out = []
    for i in range(1, 11):
        above = [b - a for a, b in zip(cells[i], cells[i + 1])]
        minus, plus = predict(cells[i], below, above, k)
        below = above
        if plus_before is not None:
            flux = face_flux(plus_before, minus, k, v_before, minus[k] / minus[0])
            if flux_before is not None:
                out.append([f - g for f, g in zip(flux, flux_before)])
            flux_before = flux
        plus_before = plus
        v_before = plus[k] / plus[0]
    return out


def across_kernel(info, acc, rem, x_low, x_high, z_low, z_high, send, part):
    lane = lanes()
    low_shift, high_shift = info[2], info[3]

    def radial(z, _):
        cells = [[ring_roll(x_low[c, x, z], low_shift, lane) for c in range(4)] for x in range(2)]
        cells += [[rem[c, x, z] for c in range(4)] for x in range(8)]
        cells += [[ring_roll(x_high[c, x, z], high_shift, lane) for c in range(4)] for x in range(2)]
        for x, div in enumerate(march(cells, 1)):
            for c in range(4):
                part[c, x, z] = acc[c, x, z] - DT * div[c]
        return 0

    lax.fori_loop(0, 8, radial, 0)
    at_bottom, at_top = info[4] == 1, info[5] == 1

    def vertical(xq, _):
        news = []
        for x in (xq, xq + 4):
            inner = [[rem[c, x, z] for c in range(4)] for z in range(8)]
            below = [[jnp.where(at_bottom, inner[0][c], z_low[c, x, z]) for c in range(4)] for z in range(2)]
            above = [[jnp.where(at_top, inner[7][c], z_high[c, x, z]) for c in range(4)] for z in range(2)]
            div = march(below + inner + above, 3)
            news.append([[part[c, x, z] - DT * div[z][c] for c in range(4)] for z in range(8)])
        for z in range(8):
            for c in range(4):
                base = (c * 4 + xq) * 8 + z
                one, two = news[0][z][c], news[1][z][c]
                send[pl.ds(base, 8, stride=256), :] = jnp.where(lane < 64, one, pltpu.roll(two, 64, 1))
                send[pl.ds(base + 128, 8, stride=256), :] = jnp.where(lane < 64, pltpu.roll(one, 64, 1), two)
        return 0

    lax.fori_loop(0, 4, vertical, 0)


def on_device(density, momentum, column_shift, column_fraction, shear_offset):
    gx, gy, gz = lax.axis_index("gx"), lax.axis_index("gy"), lax.axis_index("gz")
    path = jnp.asarray(np.array(PATH, np.int32))
    place = jnp.asarray(np.argsort(np.array(PATH)).astype(np.int32))
    dest = jnp.where(gz == 0, path, path[::-1])
    chunk = jnp.where(gz == 0, place[gy], CHUNKS - 1 - place[gy])
    offset = shear_offset[0]
    low_shift = jnp.where(gx == 0, offset, 0)
    high_shift = jnp.where(gx == 7, lax.rem(1024 - offset, 1024), 0)
    at_bottom = jnp.logical_and(gz == 0, chunk == 0).astype(jnp.int32)
    at_top = jnp.logical_and(gz == 1, chunk == CHUNKS - 1).astype(jnp.int32)
    info = jnp.stack([gx, gz * 128 + chunk * 8, low_shift, high_shift, at_bottom, at_top]).astype(jnp.int32)

    tile = lambda *lead: jax.ShapeDtypeStruct(lead + (8, 128), F32)
    send = pl.pallas_call(
        pack_kernel,
        out_shape=tile(16, 4, 4),
        in_specs=[smem(), vmem(), vmem()],
        out_specs=vmem(),
        compiler_params=params(),
        name="pack",
    )(dest, density, momentum)
    recv = lax.all_to_all(send, "gy", 0, 0)
    rem, x_low, x_high, z_low, z_high = pl.pallas_call(
        remap_kernel,
        out_shape=(tile(4, 8, 8), tile(4, 2, 8), tile(4, 2, 8), tile(4, 8, 2), tile(4, 8, 2)),
        in_specs=[smem(), smem(), smem(), vmem()],
        out_specs=(vmem(),) * 5,
        compiler_params=params(),
        name="remap",
    )(info, column_shift, column_fraction, recv.reshape(2048, 128))

    up = [(i, (i + 1) % 8) for i in range(8)]
    from_below = lax.ppermute(x_high, "gx", up)
    from_above = lax.ppermute(x_low, "gx", [(b, a) for a, b in up])
    column = [i * 2 for i in PATH] + [i * 2 + 1 for i in PATH[::-1]]
    rise = list(zip(column[:-1], column[1:]))
    from_under = lax.ppermute(z_high, ("gy", "gz"), rise)
    from_over = lax.ppermute(z_low, ("gy", "gz"), [(b, a) for a, b in rise])

    acc = pl.pallas_call(
        along_kernel,
        out_shape=tile(4, 8, 8),
        in_specs=[smem(), vmem()],
        out_specs=vmem(),
        compiler_params=params(),
        cost_estimate=pl.CostEstimate(flops=20_000_000, bytes_accessed=2 << 20, transcendentals=0),
        name="along",
    )(info, rem)
    send = pl.pallas_call(
        across_kernel,
        out_shape=jax.ShapeDtypeStruct((2048, 128), F32),
        in_specs=[smem()] + [vmem()] * 6,
        out_specs=vmem(),
        scratch_shapes=[pltpu.VMEM((4, 8, 8, 8, 128), F32)],
        compiler_params=params(),
        name="across",
    )(info, acc, rem, from_below, from_above, from_under, from_over)
    recv = lax.all_to_all(send.reshape(16, 4, 4, 8, 128), "gy", 0, 0)
    return pl.pallas_call(
        unpack_kernel,
        out_shape=(jax.ShapeDtypeStruct(density.shape, F32), jax.ShapeDtypeStruct(momentum.shape, F32)),
        in_specs=[smem(), vmem()],
        out_specs=(vmem(), vmem()),
        compiler_params=params(),
        name="unpack",
    )(dest, recv)


def solution(mesh):
    in_specs = (P("gx", "gy", "gz"), P(None, "gx", "gy", "gz"), P(), P(), P())
    out_specs = (P("gx", "gy", "gz"), P(None, "gx", "gy", "gz"))
    return jax.shard_map(
        on_device, mesh=mesh, in_specs=in_specs, out_specs=out_specs, check_vma=False
    )
```

```python
import jax
import jax.numpy as jnp
from jax import lax
from jax.experimental import pallas as pl
from jax.experimental.pallas import tpu as pltpu
from jax.sharding import PartitionSpec as P

CHIPS = [(y, 0) for y in range(4)] + [(y, 1) for y in (3, 2, 1, 0)]
PATH = [y * 4 + xh * 2 + core for y, xh in CHIPS for core in (0, 1)]
PAIRS = [(0, 4), (1, 5), (2, 6), (3, 7)]
DT = 0.15
F32 = jnp.float32


def vmem():
    return pl.BlockSpec(memory_space=pltpu.VMEM)


def smem():
    return pl.BlockSpec(memory_space=pltpu.SMEM)


def place_of():
    gy = lax.axis_index("gy")
    return lax.shift_right_logical(gy, 2), lax.shift_right_logical(gy, 1) & 1, gy & 1, lax.axis_index("gz")


def owners():
    gz = lax.axis_index("gz")
    return [jnp.where(gz == 0, a, b) for a, b in zip(PATH, PATH[::-1])]


def column_copies(q, density, momentum, held, sems, outward):
    copies = []
    for n, x in enumerate(PAIRS[q]):
        ends = [(density.at[x], held.at[q, n, 0]), (momentum.at[:, x], held.at[q, n, pl.ds(1, 3)])]
        for j, (far, near) in enumerate(ends):
            source, target = (near, far) if outward else (far, near)
            copies.append(pltpu.make_async_copy(source, target, sems.at[q, 2 * n + j]))
    return copies


def pack_kernel(density, momentum, send, held, sems):
    copies = [column_copies(q, density, momentum, held, sems, False) for q in range(4)]
    for group in copies:
        for copy in group:
            copy.start()
    to = owners()
    for q in range(4):
        for copy in copies[q]:
            copy.wait()
        for c in range(4):
            turned = jnp.concatenate([held[q, 0, c], held[q, 1, c]], axis=0).T
            for k, device in enumerate(to):
                send[device, c, q] = turned[8 * k : 8 * k + 8]


def unpack_kernel(recv, density, momentum, held, sems):
    copies = [column_copies(q, density, momentum, held, sems, True) for q in range(4)]
    given = owners()
    for q in range(4):
        for c in range(4):
            turned = jnp.concatenate([recv[device, c, q] for device in given], axis=0).T
            held[q, 0, c] = turned[:64]
            held[q, 1, c] = turned[64:]
        for copy in copies[q]:
            copy.start()
    for group in copies:
        for copy in group:
            copy.wait()


def lanes():
    return lax.broadcasted_iota(jnp.int32, (8, 128), 1)


def ring_roll(tile, shift, lane):
    far, near = shift // 128, shift % 128
    turned = pltpu.roll(tile, near, 1)
    return jnp.where(lane < near, pltpu.roll(turned, far + 1, 0), pltpu.roll(turned, far, 0))


def ring_next(tile, lane):
    turned = pltpu.roll(tile, 127, 1)
    return jnp.where(lane == 127, pltpu.roll(turned, 7, 0), turned)


def ring_prev(tile, lane):
    turned = pltpu.roll(tile, 1, 1)
    return jnp.where(lane == 0, pltpu.roll(turned, 1, 0), turned)


def remap_kernel(shifts, fractions, recv, rem, x_low, x_high, z_inner, z_outer):
    lane = lanes()
    first = lax.axis_index("gx") * 8
    _, _, core, gz = place_of()
    inner_is_high = (core ^ gz) == 0

    def one(c, _):
        for q, columns in enumerate(PAIRS):
            shift = [shifts[first + x] for x in columns]
            weight = [fractions[first + x] for x in columns]
            ends = {}
            for z in range(8):
                base = (c * 4 + q) * 8 + z
                even = recv[pl.ds(base, 8, stride=256), :]
                odd = recv[pl.ds(base + 128, 8, stride=256), :]
                tiles = (
                    jnp.where(lane < 64, even, pltpu.roll(odd, 64, 1)),
                    jnp.where(lane < 64, pltpu.roll(even, 64, 1), odd),
                )
                for i, x in enumerate(columns):
                    mixed = (1.0 - weight[i]) * tiles[i] + weight[i] * ring_prev(tiles[i], lane)
                    value = ring_roll(mixed, shift[i], lane)
                    rem[c, x, z] = value
                    ends[x, z] = value
                    if x < 2:
                        x_low[c, x, z] = value
                    if x >= 6:
                        x_high[c, x - 6, z] = value
            for x in columns:
                for g in range(2):
                    z_inner[c, x, g] = jnp.where(inner_is_high, ends[x, 6 + g], ends[x, g])
                    z_outer[c, x, g] = jnp.where(inner_is_high, ends[x, g], ends[x, 6 + g])
        return 0

    lax.fori_loop(0, 4, one, 0)


def minmod(a, b):
    return jnp.maximum(jnp.minimum(a, b), 0.0) + jnp.minimum(jnp.maximum(a, b), 0.0)


def inverse(a):
    first = pl.reciprocal(a, approx=True)
    return first * (2.0 - a * first)


def predict(cell, below, above, k):
    slope = [minmod(below[c], above[c]) for c in range(4)]
    half = [0.5 * s for s in slope]
    minus = [cell[c] - half[c] for c in range(4)]
    plus = [cell[c] + half[c] for c in range(4)]
    v_minus = minus[k] * inverse(minus[0])
    v_plus = plus[k] * inverse(plus[0])
    change = [0.075 * slope[k]]
    for c in range(1, 4):
        term = plus[c] * v_plus - minus[c] * v_minus
        if c == k:
            term = term + slope[0]
        change.append(0.075 * term)
    return [minus[c] - change[c] for c in range(4)], [plus[c] - change[c] for c in range(4)]


def face_flux(left, right, k, v_left, v_right):
    slowest = jnp.minimum(jnp.minimum(v_left, v_right) - 1.0, 0.0)
    fastest = jnp.maximum(jnp.maximum(v_left, v_right) + 1.0, 0.0)
    scale = inverse(fastest - slowest)
    up = fastest * scale
    down = -slowest * scale
    mix = fastest * slowest * scale
    from_left = up * v_left - mix
    from_right = down * v_right + mix
    flux = [left[c] * from_left + right[c] * from_right for c in range(4)]
    flux[k] = flux[k] + (up * left[0] + down * right[0])
    return flux


def along_kernel(rem, acc):
    lane = lanes()
    y, xh, core, gz = place_of()
    place = 2 * jnp.where(xh == 0, y, 7 - y) + core
    base = 128 * gz + 8 * jnp.where(gz == 0, place, 15 - place)

    def one(x, _):
        for z in range(8):
            cell = [rem[c, x, z] for c in range(4)]
            below = [u - ring_prev(u, lane) for u in cell]
            above = [ring_next(d, lane) for d in below]
            minus, plus = predict(cell, below, above, 2)
            v_minus = minus[2] * inverse(minus[0])
            v_plus = plus[2] * inverse(plus[0])
            right = [ring_next(m, lane) for m in minus]
            flux = face_flux(plus, right, 2, v_plus, ring_next(v_minus, lane))
            div = [f - ring_prev(f, lane) for f in flux]
            height = ((base + z).astype(F32) + (0.5 - 128.0)) * (1.0 / 128.0)
            acc[0, x, z] = cell[0] - DT * div[0]
            acc[1, x, z] = cell[1] - DT * (div[1] - 2.0 * cell[2])
            acc[2, x, z] = cell[2] - DT * (div[2] + 0.5 * cell[1])
            acc[3, x, z] = cell[3] - DT * (div[3] + height * cell[0])
        return 0

    lax.fori_loop(0, 8, one, 0)


def march(cells, k):
    flux_before = None
    plus_before = v_before = None
    below = [b - a for a, b in zip(cells[0], cells[1])]
    out = []
    for i in range(1, len(cells) - 1):
        above = [b - a for a, b in zip(cells[i], cells[i + 1])]
        minus, plus = predict(cells[i], below, above, k)
        below = above
        if plus_before is not None:
            flux = face_flux(plus_before, minus, k, v_before, minus[k] * inverse(minus[0]))
            if flux_before is not None:
                out.append([f - g for f, g in zip(flux, flux_before)])
            flux_before = flux
        plus_before = plus
        v_before = plus[k] * inverse(plus[0])
    return out


def vertical_kernel(acc, rem, from_inner, from_outer, part):
    y, xh, core, gz = place_of()
    inner_is_high = (core ^ gz) == 0
    at_end = (y | xh | core) == 0

    def one(x, _):
        inner = [[rem[c, x, z] for c in range(4)] for z in range(8)]
        below, above = [], []
        for g in range(2):
            low, high = [], []
            for c in range(4):
                near, far = from_inner[c, x, g], from_outer[c, x, g]
                end = jnp.where(inner_is_high, inner[0][c], inner[7][c])
                far = jnp.where(at_end, end, far)
                low.append(jnp.where(inner_is_high, far, near))
                high.append(jnp.where(inner_is_high, near, far))
            below.append(low)
            above.append(high)
        for z, div in enumerate(march(below + inner + above, 3)):
            for c in range(4):
                part[c, x, z] = acc[c, x, z] - DT * div[c]
        return 0

    lax.fori_loop(0, 8, one, 0)


def radial_kernel(offset, part, rem, from_below, from_above, send):
    lane = lanes()
    gx = lax.axis_index("gx")
    low_shift = jnp.where(gx == 0, offset[0], 0)
    high_shift = jnp.where(gx == 7, (1024 - offset[0]) & 1023, 0)

    def one(z, _):
        cells = [[ring_roll(from_below[c, x, z], low_shift, lane) for c in range(4)] for x in range(2)]
        cells += [[rem[c, x, z] for c in range(4)] for x in range(8)]
        cells += [[ring_roll(from_above[c, x, z], high_shift, lane) for c in range(4)] for x in range(2)]
        div = march(cells, 1)
        for q, (xa, xb) in enumerate(PAIRS):
            for c in range(4):
                base = (c * 4 + q) * 8 + z
                a, b = (part[c, x, z] - DT * div[x][c] for x in (xa, xb))
                send[pl.ds(base, 8, stride=256), :] = jnp.where(lane < 64, a, pltpu.roll(b, 64, 1))
                send[pl.ds(base + 128, 8, stride=256), :] = jnp.where(lane < 64, pltpu.roll(a, 64, 1), b)
        return 0

    lax.fori_loop(0, 8, one, 0)


def kernel_call(kernel, name, given, results, scratch=(), spaces=None, out_spaces=None, limit=48):
    return pl.pallas_call(
        kernel,
        out_shape=results,
        in_specs=spaces or [vmem()] * len(given),
        out_specs=out_spaces or (vmem(),) * len(results),
        scratch_shapes=list(scratch),
        compiler_params=pltpu.CompilerParams(vmem_limit_bytes=limit << 20),
        cost_estimate=pl.CostEstimate(flops=1000, bytes_accessed=1000, transcendentals=0),
        name=name,
    )(*given)


def on_device(density, momentum, column_shift, column_fraction, shear_offset):
    tile = lambda *lead: jax.ShapeDtypeStruct(lead + (8, 128), F32)
    far = pl.BlockSpec(memory_space=pl.ANY)
    moving = [pltpu.VMEM((4, 2, 4, 64, 128), F32), pltpu.SemaphoreType.DMA((4, 4))]
    (send,) = kernel_call(
        pack_kernel, "pack", (density, momentum), (tile(16, 4, 4),), moving, spaces=[far, far], limit=60
    )
    recv = lax.all_to_all(send, "gy", 0, 0)
    rem, x_low, x_high, z_inner, z_outer = kernel_call(
        remap_kernel,
        "remap",
        (column_shift, column_fraction, recv.reshape(2048, 128)),
        (tile(4, 8, 8), tile(4, 2, 8), tile(4, 2, 8), tile(4, 8, 2), tile(4, 8, 2)),
        spaces=[smem(), smem(), vmem()],
    )
    up = [(i, (i + 1) % 8) for i in range(8)]
    from_below = lax.ppermute(x_high, "gx", up)
    from_above = lax.ppermute(x_low, "gx", [(b, a) for a, b in up])
    from_inner = lax.ppermute(z_inner, "gy", [(i, i ^ 1) for i in range(16)])
    outer = [(2 * a + g, 2 * b + g) for a, b in zip(PATH[1:-1:2], PATH[2:-1:2]) for g in (0, 1)]
    outer.append((2 * PATH[-1], 2 * PATH[-1] + 1))
    from_outer = lax.ppermute(z_outer, ("gy", "gz"), outer + [(b, a) for a, b in outer])

    (acc,) = kernel_call(along_kernel, "along", (rem,), (tile(4, 8, 8),))
    (part,) = kernel_call(vertical_kernel, "vertical", (acc, rem, from_inner, from_outer), (tile(4, 8, 8),))
    (send,) = kernel_call(
        radial_kernel,
        "radial",
        (shear_offset, part, rem, from_below, from_above),
        (jax.ShapeDtypeStruct((2048, 128), F32),),
        spaces=[smem()] + [vmem()] * 4,
    )
    recv = lax.all_to_all(send.reshape(16, 4, 4, 8, 128), "gy", 0, 0)
    return kernel_call(
        unpack_kernel,
        "unpack",
        (recv,),
        (jax.ShapeDtypeStruct(density.shape, F32), jax.ShapeDtypeStruct(momentum.shape, F32)),
        moving,
        out_spaces=(far, far),
    )


def solution(mesh):
    in_specs = (P("gx", "gy", "gz"), P(None, "gx", "gy", "gz"), P(), P(), P())
    out_specs = (P("gx", "gy", "gz"), P(None, "gx", "gy", "gz"))
    return jax.shard_map(
        on_device, mesh=mesh, in_specs=in_specs, out_specs=out_specs, check_vma=False
    )
```

```python
import jax
import jax.numpy as jnp
from jax import lax
from jax.experimental import pallas as pl
from jax.experimental.pallas import tpu as pltpu
from jax.sharding import PartitionSpec as P

CHIPS = [(y, 0) for y in range(4)] + [(y, 1) for y in (3, 2, 1, 0)]
PATH = [y * 4 + xh * 2 + core for y, xh in CHIPS for core in (0, 1)]
PAIRS = [(0, 4), (1, 5), (2, 6), (3, 7)]
DT = 0.15
F32 = jnp.float32


def vmem():
    return pl.BlockSpec(memory_space=pltpu.VMEM)


def place_of():
    gy = lax.axis_index("gy")
    return lax.shift_right_logical(gy, 2), lax.shift_right_logical(gy, 1) & 1, gy & 1, lax.axis_index("gz")


def owners():
    gz = lax.axis_index("gz")
    return [jnp.where(gz == 0, a, b) for a, b in zip(PATH, PATH[::-1])]


def column_copies(q, density, momentum, held, sems, outward):
    copies = []
    for n, x in enumerate(PAIRS[q]):
        ends = [(density.at[x], held.at[q, n, 0]), (momentum.at[:, x], held.at[q, n, pl.ds(1, 3)])]
        for j, (far, near) in enumerate(ends):
            source, target = (near, far) if outward else (far, near)
            copies.append(pltpu.make_async_copy(source, target, sems.at[q, 2 * n + j]))
    return copies


def pack_kernel(density, momentum, send, held, sems):
    copies = [column_copies(q, density, momentum, held, sems, False) for q in range(4)]
    for group in copies:
        for copy in group:
            copy.start()
    to = owners()
    for q in range(4):
        for copy in copies[q]:
            copy.wait()
        for c in range(4):
            turned = jnp.concatenate([held[q, 0, c], held[q, 1, c]], axis=0).T
            for k, device in enumerate(to):
                send[device, c, q] = turned[8 * k : 8 * k + 8]


def unpack_kernel(recv, density, momentum, held, sems):
    copies = [column_copies(q, density, momentum, held, sems, True) for q in range(4)]
    given = owners()
    for q in range(4):
        for c in range(4):
            turned = jnp.concatenate([recv[device, c, q] for device in given], axis=0).T
            held[q, 0, c] = turned[:64]
            held[q, 1, c] = turned[64:]
        for copy in copies[q]:
            copy.start()
    for group in copies:
        for copy in group:
            copy.wait()


def lanes():
    return lax.broadcasted_iota(jnp.int32, (8, 128), 1)


def ring_roll(tile, shift, lane):
    far, near = shift // 128, shift % 128
    turned = pltpu.roll(tile, near, 1)
    return jnp.where(lane < near, pltpu.roll(turned, far + 1, 0), pltpu.roll(turned, far, 0))


def ring_next(tile, lane):
    turned = pltpu.roll(tile, 127, 1)
    return jnp.where(lane == 127, pltpu.roll(turned, 7, 0), turned)


def ring_prev(tile, lane):
    turned = pltpu.roll(tile, 1, 1)
    return jnp.where(lane == 0, pltpu.roll(turned, 1, 0), turned)


def remap_kernel(table, weights, recv, rem, x_low, x_high, z_inner, z_outer, mixed, shifts, sem):
    fetch = pltpu.make_async_copy(table, shifts, sem)
    fetch.start()
    lane = lanes()
    _, _, core, gz = place_of()
    inner_is_high = (core ^ gz) == 0

    def mix(c, _):
        for q, columns in enumerate(PAIRS):
            weight = [weights[x] for x in columns]
            for z in range(8):
                base = (c * 4 + q) * 8 + z
                even = recv[pl.ds(base, 8, stride=256), :]
                odd = recv[pl.ds(base + 128, 8, stride=256), :]
                tiles = (
                    jnp.where(lane < 64, even, pltpu.roll(odd, 64, 1)),
                    jnp.where(lane < 64, pltpu.roll(even, 64, 1), odd),
                )
                for tile, w, x in zip(tiles, weight, columns):
                    mixed[c, x, z] = (1.0 - w) * tile + w * ring_prev(tile, lane)
        return 0

    lax.fori_loop(0, 4, mix, 0)
    fetch.wait()

    def move(c, _):
        for x in range(8):
            ends = []
            for z in range(8):
                value = ring_roll(mixed[c, x, z], shifts[x], lane)
                rem[c, x, z] = value
                if z < 2 or z >= 6:
                    ends.append(value)
                if x < 2:
                    x_low[c, x, z] = ring_roll(mixed[c, x, z], shifts[8 + x], lane)
                if x >= 6:
                    x_high[c, x - 6, z] = ring_roll(mixed[c, x, z], shifts[4 + x], lane)
            for g in range(2):
                z_inner[c, x, g] = jnp.where(inner_is_high, ends[2 + g], ends[g])
                z_outer[c, x, g] = jnp.where(inner_is_high, ends[g], ends[2 + g])
        return 0

    lax.fori_loop(0, 4, move, 0)


def minmod(a, b):
    return jnp.maximum(jnp.minimum(a, b), 0.0) + jnp.minimum(jnp.maximum(a, b), 0.0)


def inverse(a):
    first = pl.reciprocal(a, approx=True)
    return first * (2.0 - a * first)


def predict(cell, below, above, k):
    slope = [minmod(below[c], above[c]) for c in range(4)]
    half = [0.5 * s for s in slope]
    minus = [cell[c] - half[c] for c in range(4)]
    plus = [cell[c] + half[c] for c in range(4)]
    v_minus = minus[k] * inverse(minus[0])
    v_plus = plus[k] * inverse(plus[0])
    change = [0.075 * slope[k]]
    for c in range(1, 4):
        term = plus[c] * v_plus - minus[c] * v_minus
        if c == k:
            term = term + slope[0]
        change.append(0.075 * term)
    return [minus[c] - change[c] for c in range(4)], [plus[c] - change[c] for c in range(4)]


def face_flux(left, right, k, v_left, v_right):
    slowest = jnp.minimum(jnp.minimum(v_left, v_right) - 1.0, 0.0)
    fastest = jnp.maximum(jnp.maximum(v_left, v_right) + 1.0, 0.0)
    scale = inverse(fastest - slowest)
    up = fastest * scale
    down = -slowest * scale
    mix = fastest * slowest * scale
    from_left = up * v_left - mix
    from_right = down * v_right + mix
    flux = [left[c] * from_left + right[c] * from_right for c in range(4)]
    flux[k] = flux[k] + (up * left[0] + down * right[0])
    return flux


def along_kernel(rem, acc):
    lane = lanes()
    y, xh, core, gz = place_of()
    place = 2 * jnp.where(xh == 0, y, 7 - y) + core
    base = 128 * gz + 8 * jnp.where(gz == 0, place, 15 - place)
    level = base + lax.broadcasted_iota(jnp.int32, (8, 128), 0)
    height = (level.astype(F32) + (0.5 - 128.0)) * (1.0 / 128.0)

    def one(x, _):
        def rows(c, p):
            return pl.ds((c * 8 + x) * 64 + p, 8, stride=8)

        def upward(tiles):
            return [pltpu.roll(t, 1, 1) for t in tiles]

        def downward(tiles):
            return [pltpu.roll(t, 127, 1) for t in tiles]

        def first_from(here, before):
            return [jnp.where(lane == 0, b, h) for h, b in zip(here, before)]

        def last_from(here, after):
            return [jnp.where(lane == 127, b, h) for h, b in zip(here, after)]

        def load(p):
            return [rem[rows(c, p), :] for c in range(4)]

        def differ(p, before):
            cell = load(p)
            turned = upward(cell)
            below = [u - w for u, w in zip(cell, first_from(turned, before))]
            return cell, below, downward(below), turned

        def store(p, flux, before):
            cell = load(p)
            div = [f - w for f, w in zip(flux, before)]
            acc[rows(0, p), :] = cell[0] - DT * div[0]
            acc[rows(1, p), :] = cell[1] - DT * (div[1] - 2.0 * cell[2])
            acc[rows(2, p), :] = cell[2] - DT * (div[2] + 0.5 * cell[1])
            acc[rows(3, p), :] = cell[3] - DT * (div[3] + height * cell[0])

        state = differ(0, upward(load(7)))
        first_down = state[2]
        first_minus = first_flux = minus_before = plus_before = flux_turned = None
        for p in range(9):
            if p < 8:
                cell, below, down, turned = state
                if p < 7:
                    state = differ(p + 1, turned)
                above = last_from(down, state[2] if p < 7 else first_down)
                minus, plus = predict(cell, below, above, 2)
                minus_down = downward(minus)
                if p == 0:
                    first_minus = minus_down
            else:
                minus_down, plus = first_minus, None
            if p > 0:
                right = last_from(minus_before, minus_down)
                flux = face_flux(
                    plus_before,
                    right,
                    2,
                    plus_before[2] * inverse(plus_before[0]),
                    right[2] * inverse(right[0]),
                )
                up = upward(flux)
                if p == 1:
                    first_flux = flux, up
                else:
                    store(p - 1, flux, first_from(up, flux_turned))
                flux_turned = up
            minus_before, plus_before = minus_down, plus
        store(0, first_flux[0], first_from(first_flux[1], flux_turned))
        return 0

    lax.fori_loop(0, 8, one, 0, unroll=2)


def face(left, right, k):
    return face_flux(left, right, k, left[k] * inverse(left[0]), right[k] * inverse(right[0]))


def less(cell, flux):
    return [u - DT * f for u, f in zip(cell, flux)]


def more(cell, flux):
    return [u + DT * f for u, f in zip(cell, flux)]


def difference(upper, lower):
    return [a - b for a, b in zip(upper, lower)]


def march(cells, k):
    fluxes = []
    first_minus = plus_before = None
    below = difference(cells[1], cells[0])
    for i in range(1, 7):
        above = difference(cells[i + 1], cells[i])
        minus, plus = predict(cells[i], below, above, k)
        below = above
        if i == 1:
            first_minus = minus
        else:
            fluxes.append(face(plus_before, minus, k))
        plus_before = plus
    return fluxes, first_minus, plus_before


def low_end(ghosts, cells, minus, k):
    outside, inside = difference(ghosts[1], ghosts[0]), difference(cells[1], cells[0])
    between = difference(cells[0], ghosts[1])
    _, plus_ghost = predict(ghosts[1], outside, between, k)
    minus_cell, plus_cell = predict(cells[0], between, inside, k)
    return face(plus_ghost, minus_cell, k), face(plus_cell, minus, k)


def high_end(ghosts, cells, plus, k):
    outside, inside = difference(ghosts[1], ghosts[0]), difference(cells[1], cells[0])
    between = difference(ghosts[0], cells[1])
    minus_cell, plus_cell = predict(cells[1], inside, between, k)
    minus_ghost, _ = predict(ghosts[0], between, outside, k)
    return face(plus, minus_cell, k), face(plus_cell, minus_ghost, k)


def inside_kernel(acc, rem, part, x_minus, x_plus, z_minus, z_plus):
    def line(cells, values, k):
        fluxes, minus, plus = march(cells, k)
        values[1] = less(values[1], fluxes[0])
        for i in range(2, 6):
            values[i] = less(values[i], difference(fluxes[i - 1], fluxes[i - 2]))
        values[6] = more(values[6], fluxes[4])
        return values, minus, plus

    def radial(z, _):
        cells = [[rem[c, x, z] for c in range(4)] for x in range(8)]
        values = [[acc[c, x, z] for c in range(4)] for x in range(8)]
        values, minus, plus = line(cells, values, 1)
        for c in range(4):
            for x in range(8):
                part[c, x, z] = values[x][c]
            x_minus[c, z] = minus[c]
            x_plus[c, z] = plus[c]
        return 0

    def vertical(x, _):
        cells = [[rem[c, x, z] for c in range(4)] for z in range(8)]
        values = [[part[c, x, z] for c in range(4)] for z in range(8)]
        values, minus, plus = line(cells, values, 3)
        for c in range(4):
            for z in range(1, 7):
                part[c, x, z] = values[z][c]
            z_minus[c, x] = minus[c]
            z_plus[c, x] = plus[c]
        return 0

    lax.fori_loop(0, 8, radial, 0)
    lax.fori_loop(0, 8, vertical, 0)


def vertical_kernel(part, rem, z_minus, z_plus, from_inner, from_outer, ends):
    y, xh, core, gz = place_of()
    inner_is_high = (core ^ gz) == 0
    at_end = (y | xh | core) == 0

    def one(x, _):
        def at(ref, z):
            return [ref[c, x, z] for c in range(4)]

        cells = {z: at(rem, z) for z in (0, 1, 6, 7)}
        low, high = [], []
        for g in range(2):
            near, far = at(from_inner, g), at(from_outer, g)
            end = [jnp.where(inner_is_high, a, b) for a, b in zip(cells[0], cells[7])]
            far = [jnp.where(at_end, a, b) for a, b in zip(end, far)]
            low.append([jnp.where(inner_is_high, a, b) for a, b in zip(far, near)])
            high.append([jnp.where(inner_is_high, a, b) for a, b in zip(near, far)])
        below, above = low_end(low, [cells[0], cells[1]], [z_minus[c, x] for c in range(4)], 3)
        values = [less(at(part, 0), difference(above, below)), more(at(part, 1), above)]
        below, above = high_end(high, [cells[6], cells[7]], [z_plus[c, x] for c in range(4)], 3)
        values += [less(at(part, 6), below), less(at(part, 7), difference(above, below))]
        for i, value in enumerate(values):
            for c in range(4):
                ends[c, x, i] = value[c]
        return 0

    lax.fori_loop(0, 8, one, 0)


def radial_kernel(part, ends, rem, x_minus, x_plus, from_below, from_above, send):
    lane = lanes()

    def level(z, values):
        def at(ref, x):
            return [ref[c, x, z] for c in range(4)]

        below, above = low_end(
            [at(from_below, 0), at(from_below, 1)],
            [at(rem, 0), at(rem, 1)],
            [x_minus[c, z] for c in range(4)],
            1,
        )
        values[0], values[1] = less(values[0], difference(above, below)), more(values[1], above)
        below, above = high_end(
            [at(from_above, 0), at(from_above, 1)],
            [at(rem, 6), at(rem, 7)],
            [x_plus[c, z] for c in range(4)],
            1,
        )
        values[6], values[7] = less(values[6], below), less(values[7], difference(above, below))
        for q, (xa, xb) in enumerate(PAIRS):
            for c in range(4):
                base = (c * 4 + q) * 8 + z
                a, b = values[xa][c], values[xb][c]
                send[pl.ds(base, 8, stride=256), :] = jnp.where(lane < 64, a, pltpu.roll(b, 64, 1))
                send[pl.ds(base + 128, 8, stride=256), :] = jnp.where(lane < 64, pltpu.roll(a, 64, 1), b)

    def middle(z, _):
        level(z, [[part[c, x, z] for c in range(4)] for x in range(8)])
        return 0

    for i, z in enumerate((0, 1, 6, 7)):
        level(z, [[ends[c, x, i] for c in range(4)] for x in range(8)])
    lax.fori_loop(2, 6, middle, 0)


def kernel_call(kernel, name, given, results, scratch=(), spaces=None, out_spaces=None, limit=48):
    return pl.pallas_call(
        kernel,
        out_shape=results,
        in_specs=spaces or [vmem()] * len(given),
        out_specs=out_spaces or (vmem(),) * len(results),
        scratch_shapes=list(scratch),
        compiler_params=pltpu.CompilerParams(vmem_limit_bytes=limit << 20),
        cost_estimate=pl.CostEstimate(flops=1000, bytes_accessed=1000, transcendentals=0),
        name=name,
    )(*given)


def on_device(density, momentum, column_shift, column_fraction, shear_offset):
    tile = lambda *lead: jax.ShapeDtypeStruct(lead + (8, 128), F32)
    far = pl.BlockSpec(memory_space=pl.ANY)
    moving = [pltpu.VMEM((4, 2, 4, 64, 128), F32), pltpu.SemaphoreType.DMA((4, 4))]
    (send,) = kernel_call(
        pack_kernel, "pack", (density, momentum), (tile(16, 4, 4),), moving, spaces=[far, far], limit=60
    )
    recv = lax.all_to_all(send, "gy", 0, 0)
    gx, offset = lax.axis_index("gx"), shear_offset[0]
    shifts = lax.dynamic_slice(column_shift, (8 * gx,), (8,))
    leaving = jnp.concatenate(
        [shifts[:2] - jnp.where(gx == 0, offset, 0), shifts[6:] + jnp.where(gx == 7, offset, 0)]
    )
    table = jnp.concatenate([shifts, leaving & 1023, jnp.zeros((116,), jnp.int32)])
    weights = lax.dynamic_slice(column_fraction, (8 * gx,), (8,))
    weights = jnp.broadcast_to(weights[:, None, None], (8, 8, 128))
    rem, x_low, x_high, z_inner, z_outer = kernel_call(
        remap_kernel,
        "remap",
        (table, weights, recv.reshape(2048, 128)),
        (tile(4, 8, 8), tile(4, 2, 8), tile(4, 2, 8), tile(4, 8, 2), tile(4, 8, 2)),
        [
            pltpu.VMEM((4, 8, 8, 8, 128), F32),
            pltpu.SMEM((128,), jnp.int32),
            pltpu.SemaphoreType.DMA,
        ],
        spaces=[far, vmem(), vmem()],
    )
    up = [(i, (i + 1) % 8) for i in range(8)]
    from_below = lax.ppermute(x_high, "gx", up)
    from_above = lax.ppermute(x_low, "gx", [(b, a) for a, b in up])
    from_inner = lax.ppermute(z_inner, "gy", [(i, i ^ 1) for i in range(16)])
    outer = [(2 * a + g, 2 * b + g) for a, b in zip(PATH[1:-1:2], PATH[2:-1:2]) for g in (0, 1)]
    outer.append((2 * PATH[-1], 2 * PATH[-1] + 1))
    from_outer = lax.ppermute(z_outer, ("gy", "gz"), outer + [(b, a) for a, b in outer])

    (acc,) = kernel_call(
        along_kernel, "along", (rem.reshape(2048, 128),), (jax.ShapeDtypeStruct((2048, 128), F32),)
    )
    acc = acc.reshape(4, 8, 8, 8, 128)
    part, x_minus, x_plus, z_minus, z_plus = kernel_call(
        inside_kernel, "inside", (acc, rem), (tile(4, 8, 8),) + (tile(4, 8),) * 4
    )
    (ends,) = kernel_call(
        vertical_kernel, "vertical", (part, rem, z_minus, z_plus, from_inner, from_outer), (tile(4, 8, 4),)
    )
    (send,) = kernel_call(
        radial_kernel,
        "radial",
        (part, ends, rem, x_minus, x_plus, from_below, from_above),
        (jax.ShapeDtypeStruct((2048, 128), F32),),
    )
    recv = lax.all_to_all(send.reshape(16, 4, 4, 8, 128), "gy", 0, 0)
    return kernel_call(
        unpack_kernel,
        "unpack",
        (recv,),
        (jax.ShapeDtypeStruct(density.shape, F32), jax.ShapeDtypeStruct(momentum.shape, F32)),
        moving,
        out_spaces=(far, far),
    )


def solution(mesh):
    in_specs = (P("gx", "gy", "gz"), P(None, "gx", "gy", "gz"), P(), P(), P())
    out_specs = (P("gx", "gy", "gz"), P(None, "gx", "gy", "gz"))
    return jax.shard_map(
        on_device, mesh=mesh, in_specs=in_specs, out_specs=out_specs, check_vma=False
    )
```

```python
import jax
import jax.numpy as jnp
from jax import lax
from jax.experimental import pallas as pl
from jax.experimental.pallas import tpu as pltpu
from jax.sharding import PartitionSpec as P

START = 0
CHIPS = [((y + START) % 4, 0) for y in range(4)] + [((y + START) % 4, 1) for y in (3, 2, 1, 0)]
PATH = [y * 4 + xh * 2 + core for y, xh in CHIPS for core in (0, 1)]
PAIRS = [(0, 6), (1, 7), (2, 4), (3, 5)]
DT = 0.15
F32 = jnp.float32


def vmem():
    return pl.BlockSpec(memory_space=pltpu.VMEM)


def place_of():
    gy = lax.axis_index("gy")
    y = (lax.shift_right_logical(gy, 2) - START) & 3
    xh, core = lax.shift_right_logical(gy, 1) & 1, gy & 1
    return 2 * jnp.where(xh == 0, y, 7 - y) + core, core, lax.axis_index("gz")


def owners():
    gz = lax.axis_index("gz")
    return [jnp.where(gz == 0, a, b) for a, b in zip(PATH, PATH[::-1])]


def component_copies(density, momentum, held, sems, outward):
    copies = []
    for c in range(4):
        far, near = density if c == 0 else momentum.at[c - 1], held.at[c]
        source, target = (near, far) if outward else (far, near)
        copies.append(pltpu.make_async_copy(source, target, sems.at[c]))
    return copies


def pack_kernel(density, momentum, send, held, packed, sems, send_sems):
    copies = component_copies(density, momentum, held, sems, False)
    for copy in copies:
        copy.start()
    to = owners()
    leaving = []
    for c in range(4):
        copies[c].wait()
        for q, (a, b) in enumerate(PAIRS):
            turned = jnp.concatenate([held[c, a], held[c, b]], axis=0).T
            for k, device in enumerate(to):
                packed[c, device, q] = turned[8 * k : 8 * k + 8]
        leaving.append(pltpu.make_async_copy(packed.at[c], send.at[:, c], send_sems.at[c]))
        leaving[c].start()
    for copy in leaving:
        copy.wait()


def unpack_kernel(recv, density, momentum, held, sems):
    copies = component_copies(density, momentum, held, sems, True)
    given = owners()
    for c in range(4):
        for q, (a, b) in enumerate(PAIRS):
            turned = jnp.concatenate([recv[device, c, q] for device in given], axis=0).T
            held[c, a] = turned[:64]
            held[c, b] = turned[64:]
        copies[c].start()
    for copy in copies:
        copy.wait()


def lanes():
    return lax.broadcasted_iota(jnp.int32, (8, 128), 1)


def ring_roll(tile, shift, lane):
    far, near = shift // 128, shift % 128
    turned = pltpu.roll(tile, near, 1)
    return jnp.where(lane < near, pltpu.roll(turned, far + 1, 0), pltpu.roll(turned, far, 0))


def ring_next(tile, lane):
    turned = pltpu.roll(tile, 127, 1)
    return jnp.where(lane == 127, pltpu.roll(turned, 7, 0), turned)


def ring_prev(tile, lane):
    turned = pltpu.roll(tile, 1, 1)
    return jnp.where(lane == 0, pltpu.roll(turned, 1, 0), turned)


def remap_kernel(table, weights, recv, rem, x_low, x_high, z_inner, z_outer, mixed, shifts, sem):
    fetch = pltpu.make_async_copy(table, shifts, sem)
    fetch.start()
    lane = lanes()
    _, core, gz = place_of()
    inner_is_high = (core ^ gz) == 0

    def mix(c, _):
        for q, columns in enumerate(PAIRS):
            weight = [weights[x] for x in columns]
            for z in range(8):
                base = (c * 4 + q) * 8 + z
                even = recv[pl.ds(base, 8, stride=256), :]
                odd = recv[pl.ds(base + 128, 8, stride=256), :]
                tiles = (
                    jnp.where(lane < 64, even, pltpu.roll(odd, 64, 1)),
                    jnp.where(lane < 64, pltpu.roll(even, 64, 1), odd),
                )
                for tile, w, x in zip(tiles, weight, columns):
                    mixed[c, x, z] = (1.0 - w) * tile + w * ring_prev(tile, lane)
        return 0

    lax.fori_loop(0, 4, mix, 0)
    fetch.wait()

    def move(c, _):
        for x in range(8):
            ends = []
            for z in range(8):
                value = ring_roll(mixed[c, x, z], shifts[x], lane)
                rem[c, x, z] = value
                if z < 2 or z >= 6:
                    ends.append(value)
                if x < 2:
                    x_low[c, x, z] = ring_roll(mixed[c, x, z], shifts[8 + x], lane)
                if x >= 6:
                    x_high[c, x - 6, z] = ring_roll(mixed[c, x, z], shifts[4 + x], lane)
            for g in range(2):
                z_inner[c, x, g] = jnp.where(inner_is_high, ends[2 + g], ends[g])
                z_outer[c, x, g] = jnp.where(inner_is_high, ends[g], ends[2 + g])
        return 0

    lax.fori_loop(0, 4, move, 0)


def minmod(a, b):
    return jnp.maximum(jnp.minimum(a, b), 0.0) + jnp.minimum(jnp.maximum(a, b), 0.0)


def inverse(a):
    first = pl.reciprocal(a, approx=True)
    return first * (2.0 - a * first)


def predict(cell, below, above, k):
    slope = [minmod(below[c], above[c]) for c in range(4)]
    half = [0.5 * s for s in slope]
    minus = [cell[c] - half[c] for c in range(4)]
    plus = [cell[c] + half[c] for c in range(4)]
    v_minus = minus[k] * inverse(minus[0])
    v_plus = plus[k] * inverse(plus[0])
    change = [0.075 * slope[k]]
    for c in range(1, 4):
        term = plus[c] * v_plus - minus[c] * v_minus
        if c == k:
            term = term + slope[0]
        change.append(0.075 * term)
    return [minus[c] - change[c] for c in range(4)], [plus[c] - change[c] for c in range(4)]


def face_flux(left, right, k, v_left, v_right):
    slowest = jnp.minimum(jnp.minimum(v_left, v_right) - 1.0, 0.0)
    fastest = jnp.maximum(jnp.maximum(v_left, v_right) + 1.0, 0.0)
    scale = inverse(fastest - slowest)
    up = fastest * scale
    down = -slowest * scale
    mix = fastest * slowest * scale
    from_left = up * v_left - mix
    from_right = down * v_right + mix
    flux = [left[c] * from_left + right[c] * from_right for c in range(4)]
    flux[k] = flux[k] + (up * left[0] + down * right[0])
    return flux


def along_kernel(rem, acc):
    lane = lanes()
    place, _, gz = place_of()
    base = 128 * gz + 8 * jnp.where(gz == 0, place, 15 - place)
    level = base + lax.broadcasted_iota(jnp.int32, (8, 128), 0)
    height = (level.astype(F32) + (0.5 - 128.0)) * (1.0 / 128.0)

    def one(x, _):
        def rows(c, p):
            return pl.ds((c * 8 + x) * 64 + p, 8, stride=8)

        def upward(tiles):
            return [pltpu.roll(t, 1, 1) for t in tiles]

        def downward(tiles):
            return [pltpu.roll(t, 127, 1) for t in tiles]

        def first_from(here, before):
            return [jnp.where(lane == 0, b, h) for h, b in zip(here, before)]

        def last_from(here, after):
            return [jnp.where(lane == 127, b, h) for h, b in zip(here, after)]

        def load(p):
            return [rem[rows(c, p), :] for c in range(4)]

        def differ(p, before):
            cell = load(p)
            turned = upward(cell)
            below = [u - w for u, w in zip(cell, first_from(turned, before))]
            return cell, below, downward(below), turned

        def store(p, flux, before):
            cell = load(p)
            div = [f - w for f, w in zip(flux, before)]
            acc[rows(0, p), :] = cell[0] - DT * div[0]
            acc[rows(1, p), :] = cell[1] - DT * (div[1] - 2.0 * cell[2])
            acc[rows(2, p), :] = cell[2] - DT * (div[2] + 0.5 * cell[1])
            acc[rows(3, p), :] = cell[3] - DT * (div[3] + height * cell[0])

        state = differ(0, upward(load(7)))
        first_down = state[2]
        first_minus = first_flux = minus_before = plus_before = flux_turned = None
        for p in range(9):
            if p < 8:
                cell, below, down, turned = state
                if p < 7:
                    state = differ(p + 1, turned)
                above = last_from(down, state[2] if p < 7 else first_down)
                minus, plus = predict(cell, below, above, 2)
                minus_down = downward(minus)
                if p == 0:
                    first_minus = minus_down
            else:
                minus_down, plus = first_minus, None
            if p > 0:
                right = last_from(minus_before, minus_down)
                flux = face_flux(
                    plus_before,
                    right,
                    2,
                    plus_before[2] * inverse(plus_before[0]),
                    right[2] * inverse(right[0]),
                )
                up = upward(flux)
                if p == 1:
                    first_flux = flux, up
                else:
                    store(p - 1, flux, first_from(up, flux_turned))
                flux_turned = up
            minus_before, plus_before = minus_down, plus
        store(0, first_flux[0], first_from(first_flux[1], flux_turned))
        return 0

    lax.fori_loop(0, 8, one, 0, unroll=2)


def face(left, right, k):
    return face_flux(left, right, k, left[k] * inverse(left[0]), right[k] * inverse(right[0]))


def less(cell, flux):
    return [u - DT * f for u, f in zip(cell, flux)]


def more(cell, flux):
    return [u + DT * f for u, f in zip(cell, flux)]


def difference(upper, lower):
    return [a - b for a, b in zip(upper, lower)]


def march(cells, k):
    fluxes = []
    first_minus = plus_before = None
    below = difference(cells[1], cells[0])
    for i in range(1, 7):
        above = difference(cells[i + 1], cells[i])
        minus, plus = predict(cells[i], below, above, k)
        below = above
        if i == 1:
            first_minus = minus
        else:
            fluxes.append(face(plus_before, minus, k))
        plus_before = plus
    return fluxes, first_minus, plus_before


def low_end(ghosts, cells, minus, k):
    outside, inside = difference(ghosts[1], ghosts[0]), difference(cells[1], cells[0])
    between = difference(cells[0], ghosts[1])
    _, plus_ghost = predict(ghosts[1], outside, between, k)
    minus_cell, plus_cell = predict(cells[0], between, inside, k)
    return face(plus_ghost, minus_cell, k), face(plus_cell, minus, k)


def high_end(ghosts, cells, plus, k):
    outside, inside = difference(ghosts[1], ghosts[0]), difference(cells[1], cells[0])
    between = difference(ghosts[0], cells[1])
    minus_cell, plus_cell = predict(cells[1], inside, between, k)
    minus_ghost, _ = predict(ghosts[0], between, outside, k)
    return face(plus, minus_cell, k), face(plus_cell, minus_ghost, k)


def inside_kernel(acc, rem, part, x_minus, x_plus, z_minus, z_plus):
    def line(cells, values, k):
        fluxes, minus, plus = march(cells, k)
        values[1] = less(values[1], fluxes[0])
        for i in range(2, 6):
            values[i] = less(values[i], difference(fluxes[i - 1], fluxes[i - 2]))
        values[6] = more(values[6], fluxes[4])
        return values, minus, plus

    def radial(z, _):
        cells = [[rem[c, x, z] for c in range(4)] for x in range(8)]
        values = [[acc[c, x, z] for c in range(4)] for x in range(8)]
        values, minus, plus = line(cells, values, 1)
        for c in range(4):
            for x in range(8):
                part[c, x, z] = values[x][c]
            x_minus[c, z] = minus[c]
            x_plus[c, z] = plus[c]
        return 0

    def vertical(x, _):
        cells = [[rem[c, x, z] for c in range(4)] for z in range(8)]
        values = [[part[c, x, z] for c in range(4)] for z in range(8)]
        values, minus, plus = line(cells, values, 3)
        for c in range(4):
            for z in range(1, 7):
                part[c, x, z] = values[z][c]
            z_minus[c, x] = minus[c]
            z_plus[c, x] = plus[c]
        return 0

    lax.fori_loop(0, 8, radial, 0)
    lax.fori_loop(0, 8, vertical, 0)


def vertical_kernel(part, rem, z_minus, z_plus, from_inner, from_outer, ends):
    place, core, gz = place_of()
    inner_is_high = (core ^ gz) == 0
    at_end = place == 0

    def one(x, _):
        def at(ref, z):
            return [ref[c, x, z] for c in range(4)]

        cells = {z: at(rem, z) for z in (0, 1, 6, 7)}
        low, high = [], []
        for g in range(2):
            near, far = at(from_inner, g), at(from_outer, g)
            end = [jnp.where(inner_is_high, a, b) for a, b in zip(cells[0], cells[7])]
            far = [jnp.where(at_end, a, b) for a, b in zip(end, far)]
            low.append([jnp.where(inner_is_high, a, b) for a, b in zip(far, near)])
            high.append([jnp.where(inner_is_high, a, b) for a, b in zip(near, far)])
        below, above = low_end(low, [cells[0], cells[1]], [z_minus[c, x] for c in range(4)], 3)
        values = [less(at(part, 0), difference(above, below)), more(at(part, 1), above)]
        below, above = high_end(high, [cells[6], cells[7]], [z_plus[c, x] for c in range(4)], 3)
        values += [less(at(part, 6), below), less(at(part, 7), difference(above, below))]
        for i, value in enumerate(values):
            for c in range(4):
                ends[c, x, i] = value[c]
        return 0

    lax.fori_loop(0, 8, one, 0)


def radial_kernel(part, ends, rem, x_minus, x_plus, from_below, from_above, send):
    lane = lanes()

    def level(z, values):
        def at(ref, x):
            return [ref[c, x, z] for c in range(4)]

        below, above = low_end(
            [at(from_below, 0), at(from_below, 1)],
            [at(rem, 0), at(rem, 1)],
            [x_minus[c, z] for c in range(4)],
            1,
        )
        values[0], values[1] = less(values[0], difference(above, below)), more(values[1], above)
        below, above = high_end(
            [at(from_above, 0), at(from_above, 1)],
            [at(rem, 6), at(rem, 7)],
            [x_plus[c, z] for c in range(4)],
            1,
        )
        values[6], values[7] = less(values[6], below), less(values[7], difference(above, below))
        for q, (xa, xb) in enumerate(PAIRS):
            for c in range(4):
                base = (c * 4 + q) * 8 + z
                a, b = values[xa][c], values[xb][c]
                send[pl.ds(base, 8, stride=256), :] = jnp.where(lane < 64, a, pltpu.roll(b, 64, 1))
                send[pl.ds(base + 128, 8, stride=256), :] = jnp.where(lane < 64, pltpu.roll(a, 64, 1), b)

    def middle(z, _):
        level(z, [[part[c, x, z] for c in range(4)] for x in range(8)])
        return 0

    for i, z in enumerate((0, 1, 6, 7)):
        level(z, [[ends[c, x, i] for c in range(4)] for x in range(8)])
    lax.fori_loop(2, 6, middle, 0)


def kernel_call(kernel, name, given, results, scratch=(), spaces=None, out_spaces=None, limit=48):
    return pl.pallas_call(
        kernel,
        out_shape=results,
        in_specs=spaces or [vmem()] * len(given),
        out_specs=out_spaces or (vmem(),) * len(results),
        scratch_shapes=list(scratch),
        compiler_params=pltpu.CompilerParams(vmem_limit_bytes=limit << 20),
        cost_estimate=pl.CostEstimate(flops=1000, bytes_accessed=1000, transcendentals=0),
        name=name,
    )(*given)


def on_device(density, momentum, column_shift, column_fraction, shear_offset):
    tile = lambda *lead: jax.ShapeDtypeStruct(lead + (8, 128), F32)
    far = pl.BlockSpec(memory_space=pl.ANY)
    moving = [pltpu.VMEM((4, 8, 64, 128), F32), pltpu.SemaphoreType.DMA((4,))]
    (send,) = kernel_call(
        pack_kernel,
        "pack",
        (density, momentum),
        (tile(16, 4, 4),),
        [
            moving[0],
            pltpu.VMEM((4, 16, 4, 8, 128), F32),
            moving[1],
            pltpu.SemaphoreType.DMA((4,)),
        ],
        spaces=[far, far],
        out_spaces=(far,),
        limit=60,
    )
    recv = lax.all_to_all(send, "gy", 0, 0)
    gx, offset = lax.axis_index("gx"), shear_offset[0]
    shifts = lax.dynamic_slice(column_shift, (8 * gx,), (8,))
    leaving = jnp.concatenate(
        [shifts[:2] - jnp.where(gx == 0, offset, 0), shifts[6:] + jnp.where(gx == 7, offset, 0)]
    )
    table = jnp.concatenate([shifts, leaving & 1023, jnp.zeros((116,), jnp.int32)])
    weights = lax.dynamic_slice(column_fraction, (8 * gx,), (8,))
    weights = jnp.broadcast_to(weights[:, None, None], (8, 8, 128))
    rem, x_low, x_high, z_inner, z_outer = kernel_call(
        remap_kernel,
        "remap",
        (table, weights, recv.reshape(2048, 128)),
        (tile(4, 8, 8), tile(4, 2, 8), tile(4, 2, 8), tile(4, 8, 2), tile(4, 8, 2)),
        [
            pltpu.VMEM((4, 8, 8, 8, 128), F32),
            pltpu.SMEM((128,), jnp.int32),
            pltpu.SemaphoreType.DMA,
        ],
        spaces=[far, vmem(), vmem()],
    )
    up = [(i, (i + 1) % 8) for i in range(8)]
    from_below = lax.ppermute(x_high, "gx", up)
    from_above = lax.ppermute(x_low, "gx", [(b, a) for a, b in up])
    from_inner = lax.ppermute(z_inner, "gy", [(i, i ^ 1) for i in range(16)])
    outer = [(2 * a + g, 2 * b + g) for a, b in zip(PATH[1:-1:2], PATH[2:-1:2]) for g in (0, 1)]
    outer.append((2 * PATH[-1], 2 * PATH[-1] + 1))
    from_outer = lax.ppermute(z_outer, ("gy", "gz"), outer + [(b, a) for a, b in outer])

    (acc,) = kernel_call(
        along_kernel, "along", (rem.reshape(2048, 128),), (jax.ShapeDtypeStruct((2048, 128), F32),)
    )
    acc = acc.reshape(4, 8, 8, 8, 128)
    part, x_minus, x_plus, z_minus, z_plus = kernel_call(
        inside_kernel, "inside", (acc, rem), (tile(4, 8, 8),) + (tile(4, 8),) * 4
    )
    (ends,) = kernel_call(
        vertical_kernel, "vertical", (part, rem, z_minus, z_plus, from_inner, from_outer), (tile(4, 8, 4),)
    )
    (send,) = kernel_call(
        radial_kernel,
        "radial",
        (part, ends, rem, x_minus, x_plus, from_below, from_above),
        (jax.ShapeDtypeStruct((2048, 128), F32),),
    )
    recv = lax.all_to_all(send.reshape(16, 4, 4, 8, 128), "gy", 0, 0)
    return kernel_call(
        unpack_kernel,
        "unpack",
        (recv,),
        (jax.ShapeDtypeStruct(density.shape, F32), jax.ShapeDtypeStruct(momentum.shape, F32)),
        moving,
        out_spaces=(far, far),
    )


def solution(mesh):
    in_specs = (P("gx", "gy", "gz"), P(None, "gx", "gy", "gz"), P(), P(), P())
    out_specs = (P("gx", "gy", "gz"), P(None, "gx", "gy", "gz"))
    return jax.shard_map(
        on_device, mesh=mesh, in_specs=in_specs, out_specs=out_specs, check_vma=False
    )
```

```python
import jax
import jax.numpy as jnp
from jax import lax
from jax.experimental import pallas as pl
from jax.experimental.pallas import tpu as pltpu
from jax.sharding import PartitionSpec as P

def path_of(sign):
    chips = [(y, 0) for y in range(4)] + [(y, 1) for y in (3, 2, 1, 0)]
    return [sign * y % 4 * 4 + xh * 2 + core for y, xh in chips for core in (0, 1)]


PATHS = path_of(1), path_of(-1)
PAIRS = [(0, 6), (1, 7), (2, 4), (3, 5)]
DT = 0.15
F32 = jnp.float32


def vmem():
    return pl.BlockSpec(memory_space=pltpu.VMEM)


def place_of():
    gy, gz = lax.axis_index("gy"), lax.axis_index("gz")
    y = lax.shift_right_logical(gy, 2)
    y = jnp.where(gz == 0, y, -y) & 3
    xh, core = lax.shift_right_logical(gy, 1) & 1, gy & 1
    return 2 * jnp.where(xh == 0, y, 7 - y) + core, core, gz


def owners():
    gz = lax.axis_index("gz")
    return [jnp.where(gz == 0, a, b) for a, b in zip(PATHS[0], PATHS[1][::-1])]


def component_copies(density, momentum, held, sems, outward):
    copies = []
    for c in range(4):
        far, near = density if c == 0 else momentum.at[c - 1], held.at[c]
        source, target = (near, far) if outward else (far, near)
        copies.append(pltpu.make_async_copy(source, target, sems.at[c]))
    return copies


def pack_kernel(density, momentum, send, held, packed, sems, send_sems):
    copies = component_copies(density, momentum, held, sems, False)
    for copy in copies:
        copy.start()
    to = owners()
    leaving = []
    for c in range(4):
        copies[c].wait()
        for q, (a, b) in enumerate(PAIRS):
            turned = jnp.concatenate([held[c, a], held[c, b]], axis=0).T
            for k, device in enumerate(to):
                packed[c, device, q] = turned[8 * k : 8 * k + 8]
        leaving.append(pltpu.make_async_copy(packed.at[c], send.at[:, c], send_sems.at[c]))
        leaving[c].start()
    for copy in leaving:
        copy.wait()


def unpack_kernel(recv, density, momentum, held, sems):
    copies = component_copies(density, momentum, held, sems, True)
    given = owners()
    for c in range(4):
        for q, (a, b) in enumerate(PAIRS):
            turned = jnp.concatenate([recv[device, c, q] for device in given], axis=0).T
            held[c, a] = turned[:64]
            held[c, b] = turned[64:]
        copies[c].start()
    for copy in copies:
        copy.wait()


def lanes():
    return lax.broadcasted_iota(jnp.int32, (8, 128), 1)


def ring_roll(tile, shift, lane):
    far, near = shift // 128, shift % 128
    turned = pltpu.roll(tile, near, 1)
    return jnp.where(lane < near, pltpu.roll(turned, far + 1, 0), pltpu.roll(turned, far, 0))


def ring_next(tile, lane):
    turned = pltpu.roll(tile, 127, 1)
    return jnp.where(lane == 127, pltpu.roll(turned, 7, 0), turned)


def ring_prev(tile, lane):
    turned = pltpu.roll(tile, 1, 1)
    return jnp.where(lane == 0, pltpu.roll(turned, 1, 0), turned)


def remap_kernel(table, weights, recv, rem, x_first, x_second, z_inner, z_outer, mixed, shifts, sem):
    fetch = pltpu.make_async_copy(table, shifts, sem)
    fetch.start()
    lane = lanes()
    _, core, gz = place_of()
    odd = (lax.axis_index("gx") & 1) == 1
    inner_is_high = (core ^ gz) == 0

    def mix(c, _):
        for q, columns in enumerate(PAIRS):
            weight = [weights[x] for x in columns]
            for z in range(8):
                base = (c * 4 + q) * 8 + z
                even = recv[pl.ds(base, 8, stride=256), :]
                odd = recv[pl.ds(base + 128, 8, stride=256), :]
                tiles = (
                    jnp.where(lane < 64, even, pltpu.roll(odd, 64, 1)),
                    jnp.where(lane < 64, pltpu.roll(even, 64, 1), odd),
                )
                for tile, w, x in zip(tiles, weight, columns):
                    mixed[c, x, z] = (1.0 - w) * tile + w * ring_prev(tile, lane)
        return 0

    lax.fori_loop(0, 4, mix, 0)
    fetch.wait()

    def move(c, _):
        leaving = {}
        for x in range(8):
            ends = []
            for z in range(8):
                value = ring_roll(mixed[c, x, z], shifts[x], lane)
                rem[c, x, z] = value
                if z < 2 or z >= 6:
                    ends.append(value)
                if x < 2:
                    leaving[x, z] = ring_roll(mixed[c, x, z], shifts[8 + x], lane)
                if x >= 6:
                    leaving[x, z] = ring_roll(mixed[c, x, z], shifts[4 + x], lane)
            for g in range(2):
                z_inner[c, x, g] = jnp.where(inner_is_high, ends[2 + g], ends[g])
                z_outer[c, x, g] = jnp.where(inner_is_high, ends[g], ends[2 + g])
        for x in range(2):
            for z in range(8):
                x_first[c, x, z] = jnp.where(odd, leaving[6 + x, z], leaving[x, z])
                x_second[c, x, z] = jnp.where(odd, leaving[x, z], leaving[6 + x, z])
        return 0

    lax.fori_loop(0, 4, move, 0)


def minmod(a, b):
    return jnp.maximum(jnp.minimum(a, b), 0.0) + jnp.minimum(jnp.maximum(a, b), 0.0)


def inverse(a):
    first = pl.reciprocal(a, approx=True)
    return first * (2.0 - a * first)


def predict(cell, below, above, k):
    slope = [minmod(below[c], above[c]) for c in range(4)]
    half = [0.5 * s for s in slope]
    minus = [cell[c] - half[c] for c in range(4)]
    plus = [cell[c] + half[c] for c in range(4)]
    v_minus = minus[k] * inverse(minus[0])
    v_plus = plus[k] * inverse(plus[0])
    change = [0.075 * slope[k]]
    for c in range(1, 4):
        term = plus[c] * v_plus - minus[c] * v_minus
        if c == k:
            term = term + slope[0]
        change.append(0.075 * term)
    return [minus[c] - change[c] for c in range(4)], [plus[c] - change[c] for c in range(4)]


def face_flux(left, right, k, v_left, v_right):
    slowest = jnp.minimum(jnp.minimum(v_left, v_right) - 1.0, 0.0)
    fastest = jnp.maximum(jnp.maximum(v_left, v_right) + 1.0, 0.0)
    scale = inverse(fastest - slowest)
    up = fastest * scale
    down = -slowest * scale
    mix = fastest * slowest * scale
    from_left = up * v_left - mix
    from_right = down * v_right + mix
    flux = [left[c] * from_left + right[c] * from_right for c in range(4)]
    flux[k] = flux[k] + (up * left[0] + down * right[0])
    return flux


def along(rem, acc):
    lane = lanes()
    place, _, gz = place_of()
    base = 128 * gz + 8 * jnp.where(gz == 0, place, 15 - place)
    level = base + lax.broadcasted_iota(jnp.int32, (8, 128), 0)
    height = (level.astype(F32) + (0.5 - 128.0)) * (1.0 / 128.0)

    def one(x, _):
        def rows(c, p):
            return pl.ds((c * 8 + x) * 64 + p, 8, stride=8)

        def upward(tiles):
            return [pltpu.roll(t, 1, 1) for t in tiles]

        def downward(tiles):
            return [pltpu.roll(t, 127, 1) for t in tiles]

        def first_from(here, before):
            return [jnp.where(lane == 0, b, h) for h, b in zip(here, before)]

        def last_from(here, after):
            return [jnp.where(lane == 127, b, h) for h, b in zip(here, after)]

        def load(p):
            return [rem[rows(c, p), :] for c in range(4)]

        def differ(p, before):
            cell = load(p)
            turned = upward(cell)
            below = [u - w for u, w in zip(cell, first_from(turned, before))]
            return cell, below, downward(below), turned

        def store(p, flux, before):
            cell = load(p)
            div = [f - w for f, w in zip(flux, before)]
            acc[rows(0, p), :] = cell[0] - DT * div[0]
            acc[rows(1, p), :] = cell[1] - DT * (div[1] - 2.0 * cell[2])
            acc[rows(2, p), :] = cell[2] - DT * (div[2] + 0.5 * cell[1])
            acc[rows(3, p), :] = cell[3] - DT * (div[3] + height * cell[0])

        state = differ(0, upward(load(7)))
        first_down = state[2]
        first_minus = first_flux = minus_before = plus_before = flux_turned = None
        for p in range(9):
            if p < 8:
                cell, below, down, turned = state
                if p < 7:
                    state = differ(p + 1, turned)
                above = last_from(down, state[2] if p < 7 else first_down)
                minus, plus = predict(cell, below, above, 2)
                minus_down = downward(minus)
                if p == 0:
                    first_minus = minus_down
            else:
                minus_down, plus = first_minus, None
            if p > 0:
                right = last_from(minus_before, minus_down)
                flux = face_flux(
                    plus_before,
                    right,
                    2,
                    plus_before[2] * inverse(plus_before[0]),
                    right[2] * inverse(right[0]),
                )
                up = upward(flux)
                if p == 1:
                    first_flux = flux, up
                else:
                    store(p - 1, flux, first_from(up, flux_turned))
                flux_turned = up
            minus_before, plus_before = minus_down, plus
        store(0, first_flux[0], first_from(first_flux[1], flux_turned))
        return 0

    lax.fori_loop(0, 8, one, 0, unroll=2)


def face(left, right, k):
    return face_flux(left, right, k, left[k] * inverse(left[0]), right[k] * inverse(right[0]))


def less(cell, flux):
    return [u - DT * f for u, f in zip(cell, flux)]


def more(cell, flux):
    return [u + DT * f for u, f in zip(cell, flux)]


def difference(upper, lower):
    return [a - b for a, b in zip(upper, lower)]


def march(cells, k):
    fluxes = []
    first_minus = plus_before = None
    below = difference(cells[1], cells[0])
    for i in range(1, 7):
        above = difference(cells[i + 1], cells[i])
        minus, plus = predict(cells[i], below, above, k)
        below = above
        if i == 1:
            first_minus = minus
        else:
            fluxes.append(face(plus_before, minus, k))
        plus_before = plus
    return fluxes, first_minus, plus_before


def low_end(ghosts, cells, minus, k):
    outside, inside = difference(ghosts[1], ghosts[0]), difference(cells[1], cells[0])
    between = difference(cells[0], ghosts[1])
    _, plus_ghost = predict(ghosts[1], outside, between, k)
    minus_cell, plus_cell = predict(cells[0], between, inside, k)
    return face(plus_ghost, minus_cell, k), face(plus_cell, minus, k)


def high_end(ghosts, cells, plus, k):
    outside, inside = difference(ghosts[1], ghosts[0]), difference(cells[1], cells[0])
    between = difference(ghosts[0], cells[1])
    minus_cell, plus_cell = predict(cells[1], inside, between, k)
    minus_ghost, _ = predict(ghosts[0], between, outside, k)
    return face(plus, minus_cell, k), face(plus_cell, minus_ghost, k)


def inside(acc, rem, part, x_minus, x_plus, z_minus, z_plus):
    def line(cells, values, k):
        fluxes, minus, plus = march(cells, k)
        values[1] = less(values[1], fluxes[0])
        for i in range(2, 6):
            values[i] = less(values[i], difference(fluxes[i - 1], fluxes[i - 2]))
        values[6] = more(values[6], fluxes[4])
        return values, minus, plus

    def radial(z, _):
        cells = [[rem[c, x, z] for c in range(4)] for x in range(8)]
        values = [
            [acc[pl.ds(pl.multiple_of(((c * 8 + x) * 8 + z) * 8, 8), 8), :] for c in range(4)]
            for x in range(8)
        ]
        values, minus, plus = line(cells, values, 1)
        for c in range(4):
            for x in range(8):
                part[c, x, z] = values[x][c]
            x_minus[c, z] = minus[c]
            x_plus[c, z] = plus[c]
        return 0

    def vertical(x, _):
        cells = [[rem[c, x, z] for c in range(4)] for z in range(8)]
        values = [[part[c, x, z] for c in range(4)] for z in range(8)]
        values, minus, plus = line(cells, values, 3)
        for c in range(4):
            for z in range(1, 7):
                part[c, x, z] = values[z][c]
            z_minus[c, x] = minus[c]
            z_plus[c, x] = plus[c]
        return 0

    lax.fori_loop(0, 8, radial, 0)
    lax.fori_loop(0, 8, vertical, 0)


def waits_long():
    gx = lax.axis_index("gx")
    return (gx == 0) | (gx == 3)


def early_kernel(rem, rem_rows, x_first, x_second, z_inner, z_outer, *refs):
    part, x_minus, x_plus, z_minus, z_plus, first_out, second_out, inner_out, outer_out, acc = refs

    @pl.when(waits_long())
    def _():
        along(rem_rows, acc)
        inside(acc, rem, part, x_minus, x_plus, z_minus, z_plus)

    def pass_on(c, _):
        first_out[c] = x_first[c]
        second_out[c] = x_second[c]
        inner_out[c] = z_inner[c]
        outer_out[c] = z_outer[c]
        return 0

    lax.fori_loop(0, 4, pass_on, 0)


def late_kernel(rem, rem_rows, *refs):
    done, (*results, acc) = refs[:5], refs[5:]
    early = waits_long()

    @pl.when(early)
    def _():
        def pass_on(c, _):
            for given, result in zip(done, results):
                result[c] = given[c]
            return 0

        lax.fori_loop(0, 4, pass_on, 0)

    @pl.when(jnp.logical_not(early))
    def _():
        along(rem_rows, acc)
        inside(acc, rem, *results)


def radial_kernel(part, rem, x_minus, x_plus, from_first, from_second, ends):
    odd = (lax.axis_index("gx") & 1) == 1

    def one(z, _):
        def at(ref, x):
            return [ref[c, x, z] for c in range(4)]

        def ghosts(low):
            pairs = [zip(at(from_first, x), at(from_second, x)) for x in range(2)]
            return [[jnp.where(odd == low, b, a) for a, b in pair] for pair in pairs]

        below, above = low_end(
            ghosts(True),
            [at(rem, 0), at(rem, 1)],
            [x_minus[c, z] for c in range(4)],
            1,
        )
        values = [less(at(part, 0), difference(above, below)), more(at(part, 1), above)]
        below, above = high_end(
            ghosts(False),
            [at(rem, 6), at(rem, 7)],
            [x_plus[c, z] for c in range(4)],
            1,
        )
        values += [less(at(part, 6), below), less(at(part, 7), difference(above, below))]
        for i, value in enumerate(values):
            for c in range(4):
                ends[c, i, z] = value[c]
        return 0

    lax.fori_loop(0, 8, one, 0)


def vertical_kernel(part, ends, rem, z_minus, z_plus, from_outer, from_inner, send):
    lane = lanes()
    place, core, gz = place_of()
    inner_is_high = (core ^ gz) == 0
    at_end = place == 0

    def column(x, values):
        def at(z):
            return [rem[c, x, z] for c in range(4)]

        cells = {z: at(z) for z in (0, 1, 6, 7)}
        low, high = [], []
        for g in range(2):
            near = [from_inner[c, x, g] for c in range(4)]
            far = [from_outer[c, x, g] for c in range(4)]
            end = [jnp.where(inner_is_high, a, b) for a, b in zip(cells[0], cells[7])]
            far = [jnp.where(at_end, a, b) for a, b in zip(end, far)]
            low.append([jnp.where(inner_is_high, a, b) for a, b in zip(far, near)])
            high.append([jnp.where(inner_is_high, a, b) for a, b in zip(near, far)])
        below, above = low_end(low, [cells[0], cells[1]], [z_minus[c, x] for c in range(4)], 3)
        values[0], values[1] = less(values[0], difference(above, below)), more(values[1], above)
        below, above = high_end(high, [cells[6], cells[7]], [z_plus[c, x] for c in range(4)], 3)
        values[6], values[7] = less(values[6], below), less(values[7], difference(above, below))
        return values

    def pack(q, first, second):
        for z in range(8):
            for c in range(4):
                base = (c * 4 + q) * 8 + z
                a, b = first[z][c], second[z][c]
                send[pl.ds(base, 8, stride=256), :] = jnp.where(lane < 64, a, pltpu.roll(b, 64, 1))
                send[pl.ds(base + 128, 8, stride=256), :] = jnp.where(lane < 64, pltpu.roll(a, 64, 1), b)

    def outer_pair(q, _):
        pair = [
            column(x, [[ends[c, i, z] for c in range(4)] for z in range(8)])
            for x, i in ((q, q), (q + 6, q + 2))
        ]
        pack(q, *pair)
        return 0

    def inner_pair(q, _):
        pair = [column(x, [[part[c, x, z] for c in range(4)] for z in range(8)]) for x in (q, q + 2)]
        pack(q, *pair)
        return 0

    lax.fori_loop(0, 2, outer_pair, 0)
    lax.fori_loop(2, 4, inner_pair, 0)


def kernel_call(kernel, name, given, results, scratch=(), spaces=None, out_spaces=None, limit=48):
    return pl.pallas_call(
        kernel,
        out_shape=results,
        in_specs=spaces or [vmem()] * len(given),
        out_specs=out_spaces or (vmem(),) * len(results),
        scratch_shapes=list(scratch),
        compiler_params=pltpu.CompilerParams(vmem_limit_bytes=limit << 20),
        cost_estimate=pl.CostEstimate(flops=1000, bytes_accessed=1000, transcendentals=0),
        name=name,
    )(*given)


def on_device(density, momentum, column_shift, column_fraction, shear_offset):
    tile = lambda *lead: jax.ShapeDtypeStruct(lead + (8, 128), F32)
    far = pl.BlockSpec(memory_space=pl.ANY)
    moving = [pltpu.VMEM((4, 8, 64, 128), F32), pltpu.SemaphoreType.DMA((4,))]
    (send,) = kernel_call(
        pack_kernel,
        "pack",
        (density, momentum),
        (tile(16, 4, 4),),
        [
            moving[0],
            pltpu.VMEM((4, 16, 4, 8, 128), F32),
            moving[1],
            pltpu.SemaphoreType.DMA((4,)),
        ],
        spaces=[far, far],
        out_spaces=(far,),
        limit=60,
    )
    recv = lax.all_to_all(send, "gy", 0, 0)
    gx, offset = lax.axis_index("gx"), shear_offset[0]
    shifts = lax.dynamic_slice(column_shift, (8 * gx,), (8,))
    leaving = jnp.concatenate(
        [shifts[:2] - jnp.where(gx == 0, offset, 0), shifts[6:] + jnp.where(gx == 7, offset, 0)]
    )
    table = jnp.concatenate([shifts, leaving & 1023, jnp.zeros((116,), jnp.int32)])
    weights = lax.dynamic_slice(column_fraction, (8 * gx,), (8,))
    weights = jnp.broadcast_to(weights[:, None, None], (8, 8, 128))
    rem, x_first, x_second, z_inner, z_outer = kernel_call(
        remap_kernel,
        "remap",
        (table, weights, recv.reshape(2048, 128)),
        (tile(4, 8, 8), tile(4, 2, 8), tile(4, 2, 8), tile(4, 8, 2), tile(4, 8, 2)),
        [
            pltpu.VMEM((4, 8, 8, 8, 128), F32),
            pltpu.SMEM((128,), jnp.int32),
            pltpu.SemaphoreType.DMA,
        ],
        spaces=[far, vmem(), vmem()],
    )
    results = (tile(4, 8, 8),) + (tile(4, 8),) * 4
    rows = rem.reshape(2048, 128)
    *early, x_first, x_second, z_inner, z_outer = kernel_call(
        early_kernel,
        "early",
        (rem, rows, x_first, x_second, z_inner, z_outer),
        results + (tile(4, 2, 8), tile(4, 2, 8), tile(4, 8, 2), tile(4, 8, 2)),
        [pltpu.VMEM((2048, 128), F32)],
    )
    from_first = lax.ppermute(x_first, "gx", [(i, ((i - 1) ^ 1) + 1 & 7) for i in range(8)])
    from_second = lax.ppermute(x_second, "gx", [(i, i ^ 1) for i in range(8)])
    from_inner = lax.ppermute(z_inner, "gy", [(i, i ^ 1) for i in range(16)])
    outer = [(2 * a + g, 2 * b + g) for g in (0, 1) for a, b in zip(PATHS[g][1:-1:2], PATHS[g][2:-1:2])]
    outer.append((2 * PATHS[0][-1], 2 * PATHS[1][-1] + 1))
    from_outer = lax.ppermute(z_outer, ("gy", "gz"), outer + [(b, a) for a, b in outer])

    part, x_minus, x_plus, z_minus, z_plus = kernel_call(
        late_kernel, "late", (rem, rows, *early), results, [pltpu.VMEM((2048, 128), F32)]
    )
    (ends,) = kernel_call(
        radial_kernel, "radial", (part, rem, x_minus, x_plus, from_first, from_second), (tile(4, 4, 8),)
    )
    (send,) = kernel_call(
        vertical_kernel,
        "vertical",
        (part, ends, rem, z_minus, z_plus, from_outer, from_inner),
        (jax.ShapeDtypeStruct((2048, 128), F32),),
    )
    recv = lax.all_to_all(send.reshape(16, 4, 4, 8, 128), "gy", 0, 0)
    return kernel_call(
        unpack_kernel,
        "unpack",
        (recv,),
        (jax.ShapeDtypeStruct(density.shape, F32), jax.ShapeDtypeStruct(momentum.shape, F32)),
        moving,
        out_spaces=(far, far),
    )


def solution(mesh):
    in_specs = (P("gx", "gy", "gz"), P(None, "gx", "gy", "gz"), P(), P(), P())
    out_specs = (P("gx", "gy", "gz"), P(None, "gx", "gy", "gz"))
    return jax.shard_map(
        on_device, mesh=mesh, in_specs=in_specs, out_specs=out_specs, check_vma=False
    )
```

```python
import jax
import jax.numpy as jnp
from jax import lax
from jax.experimental import pallas as pl
from jax.experimental.pallas import tpu as pltpu
from jax.sharding import PartitionSpec as P

def path_of(sign):
    chips = [(y, 0) for y in range(4)] + [(y, 1) for y in (3, 2, 1, 0)]
    return [sign * y % 4 * 4 + xh * 2 + core for y, xh in chips for core in (0, 1)]


PATHS = path_of(1), path_of(-1)
PAIRS = [(0, 6), (1, 7), (2, 4), (3, 5)]
DT = 0.15
F32 = jnp.float32


def vmem():
    return pl.BlockSpec(memory_space=pltpu.VMEM)


def place_of():
    gy, gz = lax.axis_index("gy"), lax.axis_index("gz")
    y = lax.shift_right_logical(gy, 2)
    y = jnp.where(gz == 0, y, -y) & 3
    xh, core = lax.shift_right_logical(gy, 1) & 1, gy & 1
    return 2 * jnp.where(xh == 0, y, 7 - y) + core, core, gz


def owners():
    gz = lax.axis_index("gz")
    return [jnp.where(gz == 0, a, b) for a, b in zip(PATHS[0], PATHS[1][::-1])]


def component_copies(density, momentum, held, sems, outward):
    copies = []
    for c in range(4):
        far, near = density if c == 0 else momentum.at[c - 1], held.at[c]
        source, target = (near, far) if outward else (far, near)
        copies.append(pltpu.make_async_copy(source, target, sems.at[c]))
    return copies


def pack_kernel(density, momentum, send, held, packed, sems, send_sems):
    copies = component_copies(density, momentum, held, sems, False)
    for copy in copies:
        copy.start()
    to = owners()
    leaving = []
    for c in range(4):
        copies[c].wait()
        for q, (a, b) in enumerate(PAIRS):
            turned = jnp.concatenate([held[c, a], held[c, b]], axis=0).T
            for k, device in enumerate(to):
                packed[c, device, q] = turned[8 * k : 8 * k + 8]
        leaving.append(pltpu.make_async_copy(packed.at[c], send.at[:, c], send_sems.at[c]))
        leaving[c].start()
    for copy in leaving:
        copy.wait()


def unpack_kernel(recv, density, momentum, held, sems):
    copies = component_copies(density, momentum, held, sems, True)
    given = owners()
    for c in range(4):
        for q, (a, b) in enumerate(PAIRS):
            turned = jnp.concatenate([recv[device, c, q] for device in given], axis=0).T
            held[c, a] = turned[:64]
            held[c, b] = turned[64:]
        copies[c].start()
    for copy in copies:
        copy.wait()


def lanes():
    return lax.broadcasted_iota(jnp.int32, (8, 128), 1)


def ring_roll(tile, shift, lane):
    far, near = shift // 128, shift % 128
    turned = pltpu.roll(tile, near, 1)
    return jnp.where(lane < near, pltpu.roll(turned, far + 1, 0), pltpu.roll(turned, far, 0))


def ring_next(tile, lane):
    turned = pltpu.roll(tile, 127, 1)
    return jnp.where(lane == 127, pltpu.roll(turned, 7, 0), turned)


def ring_prev(tile, lane):
    turned = pltpu.roll(tile, 1, 1)
    return jnp.where(lane == 0, pltpu.roll(turned, 1, 0), turned)


def remap_kernel(table, weights, recv, rem, x_first, x_second, z_inner, z_outer, mixed, shifts, sem):
    fetch = pltpu.make_async_copy(table, shifts, sem)
    fetch.start()
    lane = lanes()
    _, core, gz = place_of()
    odd = (lax.axis_index("gx") & 1) == 1
    inner_is_high = (core ^ gz) == 0

    def mix(c, _):
        for q, columns in enumerate(PAIRS):
            weight = [weights[x] for x in columns]
            for z in range(8):
                base = (c * 4 + q) * 8 + z
                even = recv[pl.ds(base, 8, stride=256), :]
                odd = recv[pl.ds(base + 128, 8, stride=256), :]
                tiles = (
                    jnp.where(lane < 64, even, pltpu.roll(odd, 64, 1)),
                    jnp.where(lane < 64, pltpu.roll(even, 64, 1), odd),
                )
                for tile, w, x in zip(tiles, weight, columns):
                    mixed[c, x, z] = (1.0 - w) * tile + w * ring_prev(tile, lane)
        return 0

    lax.fori_loop(0, 4, mix, 0)
    fetch.wait()

    def move(c, _):
        leaving = {}
        for x in range(8):
            ends = []
            for z in range(8):
                value = ring_roll(mixed[c, x, z], shifts[x], lane)
                rem[c, x, z] = value
                if z < 2 or z >= 6:
                    ends.append(value)
                if x < 2:
                    leaving[x, z] = ring_roll(mixed[c, x, z], shifts[8 + x], lane)
                if x >= 6:
                    leaving[x, z] = ring_roll(mixed[c, x, z], shifts[4 + x], lane)
            for g in range(2):
                z_inner[c, x, g] = jnp.where(inner_is_high, ends[2 + g], ends[g])
                z_outer[c, x, g] = jnp.where(inner_is_high, ends[g], ends[2 + g])
        for x in range(2):
            for z in range(8):
                x_first[c, x, z] = jnp.where(odd, leaving[6 + x, z], leaving[x, z])
                x_second[c, x, z] = jnp.where(odd, leaving[x, z], leaving[6 + x, z])
        return 0

    lax.fori_loop(0, 4, move, 0)


def minmod(a, b):
    return jnp.maximum(jnp.minimum(a, b), 0.0) + jnp.minimum(jnp.maximum(a, b), 0.0)


def inverse(a):
    first = pl.reciprocal(a, approx=True)
    return first * (2.0 - a * first)


def predict(cell, below, above, k):
    slope = [minmod(below[c], above[c]) for c in range(4)]
    half = [0.5 * s for s in slope]
    minus = [cell[c] - half[c] for c in range(4)]
    plus = [cell[c] + half[c] for c in range(4)]
    v_minus = minus[k] * inverse(minus[0])
    v_plus = plus[k] * inverse(plus[0])
    change = [0.075 * slope[k]]
    for c in range(1, 4):
        term = plus[c] * v_plus - minus[c] * v_minus
        if c == k:
            term = term + slope[0]
        change.append(0.075 * term)
    return [minus[c] - change[c] for c in range(4)], [plus[c] - change[c] for c in range(4)]


def face_flux(left, right, k, v_left, v_right):
    slowest = jnp.minimum(jnp.minimum(v_left, v_right) - 1.0, 0.0)
    fastest = jnp.maximum(jnp.maximum(v_left, v_right) + 1.0, 0.0)
    scale = inverse(fastest - slowest)
    up = fastest * scale
    down = -slowest * scale
    mix = fastest * slowest * scale
    from_left = up * v_left - mix
    from_right = down * v_right + mix
    flux = [left[c] * from_left + right[c] * from_right for c in range(4)]
    flux[k] = flux[k] + (up * left[0] + down * right[0])
    return flux


def along(rem, acc):
    lane = lanes()
    place, _, gz = place_of()
    base = 128 * gz + 8 * jnp.where(gz == 0, place, 15 - place)
    level = base + lax.broadcasted_iota(jnp.int32, (8, 128), 0)
    height = (level.astype(F32) + (0.5 - 128.0)) * (1.0 / 128.0)

    def one(x, _):
        def rows(c, p):
            return pl.ds((c * 8 + x) * 64 + p, 8, stride=8)

        def upward(tiles):
            return [pltpu.roll(t, 1, 1) for t in tiles]

        def downward(tiles):
            return [pltpu.roll(t, 127, 1) for t in tiles]

        def first_from(here, before):
            return [jnp.where(lane == 0, b, h) for h, b in zip(here, before)]

        def last_from(here, after):
            return [jnp.where(lane == 127, b, h) for h, b in zip(here, after)]

        def load(p):
            return [rem[rows(c, p), :] for c in range(4)]

        def differ(p, before):
            cell = load(p)
            turned = upward(cell)
            below = [u - w for u, w in zip(cell, first_from(turned, before))]
            return cell, below, downward(below), turned

        def store(p, flux, before):
            cell = load(p)
            div = [f - w for f, w in zip(flux, before)]
            acc[rows(0, p), :] = cell[0] - DT * div[0]
            acc[rows(1, p), :] = cell[1] - DT * (div[1] - 2.0 * cell[2])
            acc[rows(2, p), :] = cell[2] - DT * (div[2] + 0.5 * cell[1])
            acc[rows(3, p), :] = cell[3] - DT * (div[3] + height * cell[0])

        state = differ(0, upward(load(7)))
        first_down = state[2]
        first_minus = first_flux = minus_before = plus_before = flux_turned = None
        for p in range(9):
            if p < 8:
                cell, below, down, turned = state
                if p < 7:
                    state = differ(p + 1, turned)
                above = last_from(down, state[2] if p < 7 else first_down)
                minus, plus = predict(cell, below, above, 2)
                minus_down = downward(minus)
                if p == 0:
                    first_minus = minus_down
            else:
                minus_down, plus = first_minus, None
            if p > 0:
                right = last_from(minus_before, minus_down)
                flux = face_flux(
                    plus_before,
                    right,
                    2,
                    plus_before[2] * inverse(plus_before[0]),
                    right[2] * inverse(right[0]),
                )
                up = upward(flux)
                if p == 1:
                    first_flux = flux, up
                else:
                    store(p - 1, flux, first_from(up, flux_turned))
                flux_turned = up
            minus_before, plus_before = minus_down, plus
        store(0, first_flux[0], first_from(first_flux[1], flux_turned))
        return 0

    lax.fori_loop(0, 8, one, 0, unroll=2)


def face(left, right, k):
    return face_flux(left, right, k, left[k] * inverse(left[0]), right[k] * inverse(right[0]))


def less(cell, flux):
    return [u - DT * f for u, f in zip(cell, flux)]


def more(cell, flux):
    return [u + DT * f for u, f in zip(cell, flux)]


def difference(upper, lower):
    return [a - b for a, b in zip(upper, lower)]


def march(cells, k):
    fluxes = []
    first_minus = plus_before = None
    below = difference(cells[1], cells[0])
    for i in range(1, 7):
        above = difference(cells[i + 1], cells[i])
        minus, plus = predict(cells[i], below, above, k)
        below = above
        if i == 1:
            first_minus = minus
        else:
            fluxes.append(face(plus_before, minus, k))
        plus_before = plus
    return fluxes, first_minus, plus_before


def low_end(ghosts, cells, minus, k):
    outside, inside = difference(ghosts[1], ghosts[0]), difference(cells[1], cells[0])
    between = difference(cells[0], ghosts[1])
    _, plus_ghost = predict(ghosts[1], outside, between, k)
    minus_cell, plus_cell = predict(cells[0], between, inside, k)
    return face(plus_ghost, minus_cell, k), face(plus_cell, minus, k)


def high_end(ghosts, cells, plus, k):
    outside, inside = difference(ghosts[1], ghosts[0]), difference(cells[1], cells[0])
    between = difference(ghosts[0], cells[1])
    minus_cell, plus_cell = predict(cells[1], inside, between, k)
    minus_ghost, _ = predict(ghosts[0], between, outside, k)
    return face(plus, minus_cell, k), face(plus_cell, minus_ghost, k)


def inside(acc, rem, part, x_minus, x_plus, z_minus, z_plus):
    def line(cells, values, k):
        fluxes, minus, plus = march(cells, k)
        values[1] = less(values[1], fluxes[0])
        for i in range(2, 6):
            values[i] = less(values[i], difference(fluxes[i - 1], fluxes[i - 2]))
        values[6] = more(values[6], fluxes[4])
        return values, minus, plus

    def radial(z, _):
        cells = [[rem[c, x, z] for c in range(4)] for x in range(8)]
        values = [
            [acc[pl.ds(pl.multiple_of(((c * 8 + x) * 8 + z) * 8, 8), 8), :] for c in range(4)]
            for x in range(8)
        ]
        values, minus, plus = line(cells, values, 1)
        for c in range(4):
            for x in range(8):
                part[c, x, z] = values[x][c]
            x_minus[c, z] = minus[c]
            x_plus[c, z] = plus[c]
        return 0

    def vertical(x, _):
        cells = [[rem[c, x, z] for c in range(4)] for z in range(8)]
        values = [[part[c, x, z] for c in range(4)] for z in range(8)]
        values, minus, plus = line(cells, values, 3)
        for c in range(4):
            for z in range(1, 7):
                part[c, x, z] = values[z][c]
            z_minus[c, x] = minus[c]
            z_plus[c, x] = plus[c]
        return 0

    lax.fori_loop(0, 8, radial, 0)
    lax.fori_loop(0, 8, vertical, 0)


def waits_long():
    return lax.axis_index("gx") == 0


def early_kernel(rem, rem_rows, x_first, x_second, z_inner, z_outer, *refs):
    part, x_minus, x_plus, z_minus, z_plus, first_out, second_out, inner_out, outer_out, acc = refs

    @pl.when(waits_long())
    def _():
        along(rem_rows, acc)
        inside(acc, rem, part, x_minus, x_plus, z_minus, z_plus)

    def pass_on(c, _):
        first_out[c] = x_first[c]
        second_out[c] = x_second[c]
        inner_out[c] = z_inner[c]
        outer_out[c] = z_outer[c]
        return 0

    lax.fori_loop(0, 4, pass_on, 0)


def late_kernel(rem, rem_rows, *refs):
    done, (*results, acc) = refs[:5], refs[5:]
    early = waits_long()

    @pl.when(early)
    def _():
        def pass_on(c, _):
            for given, result in zip(done, results):
                result[c] = given[c]
            return 0

        lax.fori_loop(0, 4, pass_on, 0)

    @pl.when(jnp.logical_not(early))
    def _():
        along(rem_rows, acc)
        inside(acc, rem, *results)


def radial_kernel(part, rem, x_minus, x_plus, from_first, from_second, ends):
    odd = (lax.axis_index("gx") & 1) == 1

    def one(z, _):
        def at(ref, x):
            return [ref[c, x, z] for c in range(4)]

        def ghosts(low):
            pairs = [zip(at(from_first, x), at(from_second, x)) for x in range(2)]
            return [[jnp.where(odd == low, b, a) for a, b in pair] for pair in pairs]

        below, above = low_end(
            ghosts(True),
            [at(rem, 0), at(rem, 1)],
            [x_minus[c, z] for c in range(4)],
            1,
        )
        values = [less(at(part, 0), difference(above, below)), more(at(part, 1), above)]
        below, above = high_end(
            ghosts(False),
            [at(rem, 6), at(rem, 7)],
            [x_plus[c, z] for c in range(4)],
            1,
        )
        values += [less(at(part, 6), below), less(at(part, 7), difference(above, below))]
        for i, value in enumerate(values):
            for c in range(4):
                ends[c, i, z] = value[c]
        return 0

    lax.fori_loop(0, 8, one, 0)


def vertical_kernel(part, ends, rem, z_minus, z_plus, from_outer, from_inner, send):
    lane = lanes()
    place, core, gz = place_of()
    inner_is_high = (core ^ gz) == 0
    at_end = place == 0

    def column(x, values):
        def at(z):
            return [rem[c, x, z] for c in range(4)]

        cells = {z: at(z) for z in (0, 1, 6, 7)}
        low, high = [], []
        for g in range(2):
            near = [from_inner[c, x, g] for c in range(4)]
            far = [from_outer[c, x, g] for c in range(4)]
            end = [jnp.where(inner_is_high, a, b) for a, b in zip(cells[0], cells[7])]
            far = [jnp.where(at_end, a, b) for a, b in zip(end, far)]
            low.append([jnp.where(inner_is_high, a, b) for a, b in zip(far, near)])
            high.append([jnp.where(inner_is_high, a, b) for a, b in zip(near, far)])
        below, above = low_end(low, [cells[0], cells[1]], [z_minus[c, x] for c in range(4)], 3)
        values[0], values[1] = less(values[0], difference(above, below)), more(values[1], above)
        below, above = high_end(high, [cells[6], cells[7]], [z_plus[c, x] for c in range(4)], 3)
        values[6], values[7] = less(values[6], below), less(values[7], difference(above, below))
        return values

    def pack(q, first, second):
        for z in range(8):
            for c in range(4):
                base = (c * 4 + q) * 8 + z
                a, b = first[z][c], second[z][c]
                send[pl.ds(base, 8, stride=256), :] = jnp.where(lane < 64, a, pltpu.roll(b, 64, 1))
                send[pl.ds(base + 128, 8, stride=256), :] = jnp.where(lane < 64, pltpu.roll(a, 64, 1), b)

    def outer_pair(q, _):
        pair = [
            column(x, [[ends[c, i, z] for c in range(4)] for z in range(8)])
            for x, i in ((q, q), (q + 6, q + 2))
        ]
        pack(q, *pair)
        return 0

    def inner_pair(q, _):
        pair = [column(x, [[part[c, x, z] for c in range(4)] for z in range(8)]) for x in (q, q + 2)]
        pack(q, *pair)
        return 0

    lax.fori_loop(0, 2, outer_pair, 0)
    lax.fori_loop(2, 4, inner_pair, 0)


def kernel_call(kernel, name, given, results, scratch=(), spaces=None, out_spaces=None, limit=48):
    return pl.pallas_call(
        kernel,
        out_shape=results,
        in_specs=spaces or [vmem()] * len(given),
        out_specs=out_spaces or (vmem(),) * len(results),
        scratch_shapes=list(scratch),
        compiler_params=pltpu.CompilerParams(vmem_limit_bytes=limit << 20),
        cost_estimate=pl.CostEstimate(flops=1000, bytes_accessed=1000, transcendentals=0),
        name=name,
    )(*given)


def on_device(density, momentum, column_shift, column_fraction, shear_offset):
    tile = lambda *lead: jax.ShapeDtypeStruct(lead + (8, 128), F32)
    far = pl.BlockSpec(memory_space=pl.ANY)
    moving = [pltpu.VMEM((4, 8, 64, 128), F32), pltpu.SemaphoreType.DMA((4,))]
    (send,) = kernel_call(
        pack_kernel,
        "pack",
        (density, momentum),
        (tile(16, 4, 4),),
        [
            moving[0],
            pltpu.VMEM((4, 16, 4, 8, 128), F32),
            moving[1],
            pltpu.SemaphoreType.DMA((4,)),
        ],
        spaces=[far, far],
        out_spaces=(far,),
        limit=60,
    )
    recv = lax.all_to_all(send, "gy", 0, 0)
    gx, offset = lax.axis_index("gx"), shear_offset[0]
    shifts = lax.dynamic_slice(column_shift, (8 * gx,), (8,))
    leaving = jnp.concatenate(
        [shifts[:2] - jnp.where(gx == 0, offset, 0), shifts[6:] + jnp.where(gx == 7, offset, 0)]
    )
    table = jnp.concatenate([shifts, leaving & 1023, jnp.zeros((116,), jnp.int32)])
    weights = lax.dynamic_slice(column_fraction, (8 * gx,), (8,))
    weights = jnp.broadcast_to(weights[:, None, None], (8, 8, 128))
    rem, x_first, x_second, z_inner, z_outer = kernel_call(
        remap_kernel,
        "remap",
        (table, weights, recv.reshape(2048, 128)),
        (tile(4, 8, 8), tile(4, 2, 8), tile(4, 2, 8), tile(4, 8, 2), tile(4, 8, 2)),
        [
            pltpu.VMEM((4, 8, 8, 8, 128), F32),
            pltpu.SMEM((128,), jnp.int32),
            pltpu.SemaphoreType.DMA,
        ],
        spaces=[far, vmem(), vmem()],
    )
    results = (tile(4, 8, 8),) + (tile(4, 8),) * 4
    rows = rem.reshape(2048, 128)
    *early, x_first, x_second, z_inner, z_outer = kernel_call(
        early_kernel,
        "early",
        (rem, rows, x_first, x_second, z_inner, z_outer),
        results + (tile(4, 2, 8), tile(4, 2, 8), tile(4, 8, 2), tile(4, 8, 2)),
        [pltpu.VMEM((2048, 128), F32)],
    )
    from_first = lax.ppermute(x_first, "gx", [(i, ((i - 1) ^ 1) + 1 & 7) for i in range(8)])
    from_second = lax.ppermute(x_second, "gx", [(i, i ^ 1) for i in range(8)])
    from_inner = lax.ppermute(z_inner, "gy", [(i, i ^ 1) for i in range(16)])
    outer = [(2 * a + g, 2 * b + g) for g in (0, 1) for a, b in zip(PATHS[g][1:-1:2], PATHS[g][2:-1:2])]
    outer.append((2 * PATHS[0][-1], 2 * PATHS[1][-1] + 1))
    from_outer = lax.ppermute(z_outer, ("gy", "gz"), outer + [(b, a) for a, b in outer])

    part, x_minus, x_plus, z_minus, z_plus = kernel_call(
        late_kernel, "late", (rem, rows, *early), results, [pltpu.VMEM((2048, 128), F32)]
    )
    (ends,) = kernel_call(
        radial_kernel, "radial", (part, rem, x_minus, x_plus, from_first, from_second), (tile(4, 4, 8),)
    )
    (send,) = kernel_call(
        vertical_kernel,
        "vertical",
        (part, ends, rem, z_minus, z_plus, from_outer, from_inner),
        (jax.ShapeDtypeStruct((2048, 128), F32),),
    )
    recv = lax.all_to_all(send.reshape(16, 4, 4, 8, 128), "gy", 0, 0)
    return kernel_call(
        unpack_kernel,
        "unpack",
        (recv,),
        (jax.ShapeDtypeStruct(density.shape, F32), jax.ShapeDtypeStruct(momentum.shape, F32)),
        moving,
        out_spaces=(far, far),
    )


def solution(mesh):
    in_specs = (P("gx", "gy", "gz"), P(None, "gx", "gy", "gz"), P(), P(), P())
    out_specs = (P("gx", "gy", "gz"), P(None, "gx", "gy", "gz"))
    return jax.shard_map(
        on_device, mesh=mesh, in_specs=in_specs, out_specs=out_specs, check_vma=False
    )
```

```python
import jax
import jax.numpy as jnp
from jax import lax
from jax.experimental import pallas as pl
from jax.experimental.pallas import tpu as pltpu
from jax.sharding import PartitionSpec as P

def path_of(sign):
    chips = [(y, 0) for y in range(4)] + [(y, 1) for y in (3, 2, 1, 0)]
    return [sign * y % 4 * 4 + xh * 2 + core for y, xh in chips for core in (0, 1)]


PATHS = path_of(1), path_of(-1)
PAIRS = [(0, 6), (1, 7), (2, 4), (3, 5)]
DT = 0.15
F32 = jnp.float32


def vmem():
    return pl.BlockSpec(memory_space=pltpu.VMEM)


def place_of():
    gy, gz = lax.axis_index("gy"), lax.axis_index("gz")
    y = lax.shift_right_logical(gy, 2)
    y = jnp.where(gz == 0, y, -y) & 3
    xh, core = lax.shift_right_logical(gy, 1) & 1, gy & 1
    return 2 * jnp.where(xh == 0, y, 7 - y) + core, core, gz


def owners():
    gz = lax.axis_index("gz")
    return [jnp.where(gz == 0, a, b) for a, b in zip(PATHS[0], PATHS[1][::-1])]


def component_copies(density, momentum, held, sems, outward):
    copies = []
    for c in range(4):
        far, near = density if c == 0 else momentum.at[c - 1], held.at[c]
        source, target = (near, far) if outward else (far, near)
        copies.append(pltpu.make_async_copy(source, target, sems.at[c]))
    return copies


def pack_kernel(density, momentum, send, held, packed, sems, send_sems):
    copies = component_copies(density, momentum, held, sems, False)
    for copy in copies:
        copy.start()
    to = owners()
    leaving = []
    for c in range(4):
        copies[c].wait()
        for q, (a, b) in enumerate(PAIRS):
            turned = jnp.concatenate([held[c, a], held[c, b]], axis=0).T
            for k, device in enumerate(to):
                packed[c, device, q] = turned[8 * k : 8 * k + 8]
        leaving.append(pltpu.make_async_copy(packed.at[c], send.at[:, c], send_sems.at[c]))
        leaving[c].start()
    for copy in leaving:
        copy.wait()


def unpack_kernel(recv, density, momentum, held, sems):
    copies = component_copies(density, momentum, held, sems, True)
    given = owners()
    for c in range(4):
        for q, (a, b) in enumerate(PAIRS):
            turned = jnp.concatenate([recv[device, c, q] for device in given], axis=0).T
            held[c, a] = turned[:64]
            held[c, b] = turned[64:]
        copies[c].start()
    for copy in copies:
        copy.wait()


def lanes():
    return lax.broadcasted_iota(jnp.int32, (8, 128), 1)


def ring_roll(tile, shift, lane):
    far, near = shift // 128, shift % 128
    turned = pltpu.roll(tile, near, 1)
    return jnp.where(lane < near, pltpu.roll(turned, far + 1, 0), pltpu.roll(turned, far, 0))


def ring_next(tile, lane):
    turned = pltpu.roll(tile, 127, 1)
    return jnp.where(lane == 127, pltpu.roll(turned, 7, 0), turned)


def ring_prev(tile, lane):
    turned = pltpu.roll(tile, 1, 1)
    return jnp.where(lane == 0, pltpu.roll(turned, 1, 0), turned)


def remap_kernel(table, weights, recv, rem, x_first, x_second, z_inner, z_outer, mixed, shifts, sem):
    fetch = pltpu.make_async_copy(table, shifts, sem)
    fetch.start()
    lane = lanes()
    _, core, gz = place_of()
    odd = (lax.axis_index("gx") & 1) == 1
    inner_is_high = (core ^ gz) == 0

    def mix(c, _):
        for q, columns in enumerate(PAIRS):
            weight = [weights[x] for x in columns]
            for z in range(8):
                base = (c * 4 + q) * 8 + z
                even = recv[pl.ds(base, 8, stride=256), :]
                odd = recv[pl.ds(base + 128, 8, stride=256), :]
                tiles = (
                    jnp.where(lane < 64, even, pltpu.roll(odd, 64, 1)),
                    jnp.where(lane < 64, pltpu.roll(even, 64, 1), odd),
                )
                for tile, w, x in zip(tiles, weight, columns):
                    mixed[c, x, z] = (1.0 - w) * tile + w * ring_prev(tile, lane)
        return 0

    lax.fori_loop(0, 4, mix, 0)
    fetch.wait()

    def move(c, _):
        leaving = {}
        for x in range(8):
            ends = []
            for z in range(8):
                value = ring_roll(mixed[c, x, z], shifts[x], lane)
                rem[c, x, z] = value
                if z < 2 or z >= 6:
                    ends.append(value)
                if x < 2 or x >= 6:
                    leaving[x, z] = value
            for g in range(2):
                z_inner[c, x, g] = jnp.where(inner_is_high, ends[2 + g], ends[g])
                z_outer[c, x, g] = jnp.where(inner_is_high, ends[g], ends[2 + g])
        for x in range(2):
            for z in range(8):
                x_first[c, x, z] = jnp.where(odd, leaving[6 + x, z], leaving[x, z])
                x_second[c, x, z] = jnp.where(odd, leaving[x, z], leaving[6 + x, z])
        return 0

    lax.fori_loop(0, 4, move, 0)
    gx = lax.axis_index("gx")

    @pl.when((gx == 0) | (gx == 7))
    def _():
        def shear(c, _):
            for x in range(2):
                column = jnp.where(gx == 0, x, 6 + x)
                shift = shifts[jnp.where(gx == 0, 8 + x, 10 + x)]
                for z in range(8):
                    x_first[c, x, z] = ring_roll(mixed[c, column, z], shift, lane)
            return 0

        lax.fori_loop(0, 4, shear, 0)


def minmod(a, b):
    return jnp.maximum(jnp.minimum(a, b), 0.0) + jnp.minimum(jnp.maximum(a, b), 0.0)


def inverse(a):
    first = pl.reciprocal(a, approx=True)
    return first * (2.0 - a * first)


def predict(cell, below, above, k):
    slope = [minmod(below[c], above[c]) for c in range(4)]
    half = [0.5 * s for s in slope]
    minus = [cell[c] - half[c] for c in range(4)]
    plus = [cell[c] + half[c] for c in range(4)]
    v_minus = minus[k] * inverse(minus[0])
    v_plus = plus[k] * inverse(plus[0])
    change = [0.075 * slope[k]]
    for c in range(1, 4):
        term = plus[c] * v_plus - minus[c] * v_minus
        if c == k:
            term = term + slope[0]
        change.append(0.075 * term)
    return [minus[c] - change[c] for c in range(4)], [plus[c] - change[c] for c in range(4)]


def face_flux(left, right, k, v_left, v_right):
    slowest = jnp.minimum(jnp.minimum(v_left, v_right) - 1.0, 0.0)
    fastest = jnp.maximum(jnp.maximum(v_left, v_right) + 1.0, 0.0)
    scale = inverse(fastest - slowest)
    up = fastest * scale
    down = -slowest * scale
    mix = fastest * slowest * scale
    from_left = up * v_left - mix
    from_right = down * v_right + mix
    flux = [left[c] * from_left + right[c] * from_right for c in range(4)]
    flux[k] = flux[k] + (up * left[0] + down * right[0])
    return flux


def along(rem, acc):
    lane = lanes()
    place, _, gz = place_of()
    base = 128 * gz + 8 * jnp.where(gz == 0, place, 15 - place)
    level = base + lax.broadcasted_iota(jnp.int32, (8, 128), 0)
    height = (level.astype(F32) + (0.5 - 128.0)) * (1.0 / 128.0)

    def one(x, _):
        def rows(c, p):
            return pl.ds((c * 8 + x) * 64 + p, 8, stride=8)

        def upward(tiles):
            return [pltpu.roll(t, 1, 1) for t in tiles]

        def downward(tiles):
            return [pltpu.roll(t, 127, 1) for t in tiles]

        def first_from(here, before):
            return [jnp.where(lane == 0, b, h) for h, b in zip(here, before)]

        def last_from(here, after):
            return [jnp.where(lane == 127, b, h) for h, b in zip(here, after)]

        def load(p):
            return [rem[rows(c, p), :] for c in range(4)]

        def differ(p, before):
            cell = load(p)
            turned = upward(cell)
            below = [u - w for u, w in zip(cell, first_from(turned, before))]
            return cell, below, downward(below), turned

        def store(p, flux, before):
            cell = load(p)
            div = [f - w for f, w in zip(flux, before)]
            acc[rows(0, p), :] = cell[0] - DT * div[0]
            acc[rows(1, p), :] = cell[1] - DT * (div[1] - 2.0 * cell[2])
            acc[rows(2, p), :] = cell[2] - DT * (div[2] + 0.5 * cell[1])
            acc[rows(3, p), :] = cell[3] - DT * (div[3] + height * cell[0])

        state = differ(0, upward(load(7)))
        first_down = state[2]
        first_minus = first_flux = minus_before = plus_before = flux_turned = None
        for p in range(9):
            if p < 8:
                cell, below, down, turned = state
                if p < 7:
                    state = differ(p + 1, turned)
                above = last_from(down, state[2] if p < 7 else first_down)
                minus, plus = predict(cell, below, above, 2)
                minus_down = downward(minus)
                if p == 0:
                    first_minus = minus_down
            else:
                minus_down, plus = first_minus, None
            if p > 0:
                right = last_from(minus_before, minus_down)
                flux = face_flux(
                    plus_before,
                    right,
                    2,
                    plus_before[2] * inverse(plus_before[0]),
                    right[2] * inverse(right[0]),
                )
                up = upward(flux)
                if p == 1:
                    first_flux = flux, up
                else:
                    store(p - 1, flux, first_from(up, flux_turned))
                flux_turned = up
            minus_before, plus_before = minus_down, plus
        store(0, first_flux[0], first_from(first_flux[1], flux_turned))
        return 0

    lax.fori_loop(0, 8, one, 0, unroll=2)


def face(left, right, k):
    return face_flux(left, right, k, left[k] * inverse(left[0]), right[k] * inverse(right[0]))


def less(cell, flux):
    return [u - DT * f for u, f in zip(cell, flux)]


def more(cell, flux):
    return [u + DT * f for u, f in zip(cell, flux)]


def difference(upper, lower):
    return [a - b for a, b in zip(upper, lower)]


def march(cells, k):
    fluxes = []
    first_minus = plus_before = None
    below = difference(cells[1], cells[0])
    for i in range(1, 7):
        above = difference(cells[i + 1], cells[i])
        minus, plus = predict(cells[i], below, above, k)
        below = above
        if i == 1:
            first_minus = minus
        else:
            fluxes.append(face(plus_before, minus, k))
        plus_before = plus
    return fluxes, first_minus, plus_before


def low_end(ghosts, cells, minus, k):
    outside, inside = difference(ghosts[1], ghosts[0]), difference(cells[1], cells[0])
    between = difference(cells[0], ghosts[1])
    _, plus_ghost = predict(ghosts[1], outside, between, k)
    minus_cell, plus_cell = predict(cells[0], between, inside, k)
    return face(plus_ghost, minus_cell, k), face(plus_cell, minus, k)


def high_end(ghosts, cells, plus, k):
    outside, inside = difference(ghosts[1], ghosts[0]), difference(cells[1], cells[0])
    between = difference(ghosts[0], cells[1])
    minus_cell, plus_cell = predict(cells[1], inside, between, k)
    minus_ghost, _ = predict(ghosts[0], between, outside, k)
    return face(plus, minus_cell, k), face(plus_cell, minus_ghost, k)


def inside(acc, rem, part, x_minus, x_plus, z_minus, z_plus):
    def line(cells, values, k):
        fluxes, minus, plus = march(cells, k)
        values[1] = less(values[1], fluxes[0])
        for i in range(2, 6):
            values[i] = less(values[i], difference(fluxes[i - 1], fluxes[i - 2]))
        values[6] = more(values[6], fluxes[4])
        return values, minus, plus

    def radial(z, _):
        cells = [[rem[c, x, z] for c in range(4)] for x in range(8)]
        values = [
            [acc[pl.ds(pl.multiple_of(((c * 8 + x) * 8 + z) * 8, 8), 8), :] for c in range(4)]
            for x in range(8)
        ]
        values, minus, plus = line(cells, values, 1)
        for c in range(4):
            for x in range(8):
                part[c, x, z] = values[x][c]
            x_minus[c, z] = minus[c]
            x_plus[c, z] = plus[c]
        return 0

    def vertical(x, _):
        cells = [[rem[c, x, z] for c in range(4)] for z in range(8)]
        values = [[part[c, x, z] for c in range(4)] for z in range(8)]
        values, minus, plus = line(cells, values, 3)
        for c in range(4):
            for z in range(1, 7):
                part[c, x, z] = values[z][c]
            z_minus[c, x] = minus[c]
            z_plus[c, x] = plus[c]
        return 0

    lax.fori_loop(0, 8, radial, 0)
    lax.fori_loop(0, 8, vertical, 0)


def waits_long():
    return lax.axis_index("gx") == 0


def early_kernel(rem, rem_rows, x_first, x_second, z_inner, z_outer, *refs):
    part, x_minus, x_plus, z_minus, z_plus, first_out, second_out, inner_out, outer_out, acc = refs

    @pl.when(waits_long())
    def _():
        along(rem_rows, acc)
        inside(acc, rem, part, x_minus, x_plus, z_minus, z_plus)

    def pass_on(c, _):
        first_out[c] = x_first[c]
        second_out[c] = x_second[c]
        inner_out[c] = z_inner[c]
        outer_out[c] = z_outer[c]
        return 0

    lax.fori_loop(0, 4, pass_on, 0)


def late_kernel(rem, rem_rows, *refs):
    done, (*results, acc) = refs[:5], refs[5:]
    early = waits_long()

    @pl.when(early)
    def _():
        def pass_on(c, _):
            for given, result in zip(done, results):
                result[c] = given[c]
            return 0

        lax.fori_loop(0, 4, pass_on, 0)

    @pl.when(jnp.logical_not(early))
    def _():
        along(rem_rows, acc)
        inside(acc, rem, *results)


def radial_kernel(part, rem, x_minus, x_plus, from_first, from_second, ends):
    odd = (lax.axis_index("gx") & 1) == 1

    def one(z, _):
        def at(ref, x):
            return [ref[c, x, z] for c in range(4)]

        def ghosts(low):
            pairs = [zip(at(from_first, x), at(from_second, x)) for x in range(2)]
            return [[jnp.where(odd == low, b, a) for a, b in pair] for pair in pairs]

        below, above = low_end(
            ghosts(True),
            [at(rem, 0), at(rem, 1)],
            [x_minus[c, z] for c in range(4)],
            1,
        )
        values = [less(at(part, 0), difference(above, below)), more(at(part, 1), above)]
        below, above = high_end(
            ghosts(False),
            [at(rem, 6), at(rem, 7)],
            [x_plus[c, z] for c in range(4)],
            1,
        )
        values += [less(at(part, 6), below), less(at(part, 7), difference(above, below))]
        for i, value in enumerate(values):
            for c in range(4):
                ends[c, i, z] = value[c]
        return 0

    lax.fori_loop(0, 8, one, 0)


def vertical_kernel(part, ends, rem, z_minus, z_plus, from_outer, from_inner, send):
    lane = lanes()
    place, core, gz = place_of()
    inner_is_high = (core ^ gz) == 0
    at_end = place == 0

    def column(x, values):
        def at(z):
            return [rem[c, x, z] for c in range(4)]

        cells = {z: at(z) for z in (0, 1, 6, 7)}
        low, high = [], []
        for g in range(2):
            near = [from_inner[c, x, g] for c in range(4)]
            far = [from_outer[c, x, g] for c in range(4)]
            end = [jnp.where(inner_is_high, a, b) for a, b in zip(cells[0], cells[7])]
            far = [jnp.where(at_end, a, b) for a, b in zip(end, far)]
            low.append([jnp.where(inner_is_high, a, b) for a, b in zip(far, near)])
            high.append([jnp.where(inner_is_high, a, b) for a, b in zip(near, far)])
        below, above = low_end(low, [cells[0], cells[1]], [z_minus[c, x] for c in range(4)], 3)
        values[0], values[1] = less(values[0], difference(above, below)), more(values[1], above)
        below, above = high_end(high, [cells[6], cells[7]], [z_plus[c, x] for c in range(4)], 3)
        values[6], values[7] = less(values[6], below), less(values[7], difference(above, below))
        return values

    def pack(q, first, second):
        for z in range(8):
            for c in range(4):
                base = (c * 4 + q) * 8 + z
                a, b = first[z][c], second[z][c]
                send[pl.ds(base, 8, stride=256), :] = jnp.where(lane < 64, a, pltpu.roll(b, 64, 1))
                send[pl.ds(base + 128, 8, stride=256), :] = jnp.where(lane < 64, pltpu.roll(a, 64, 1), b)

    def outer_pair(q, _):
        pair = [
            column(x, [[ends[c, i, z] for c in range(4)] for z in range(8)])
            for x, i in ((q, q), (q + 6, q + 2))
        ]
        pack(q, *pair)
        return 0

    def inner_pair(q, _):
        pair = [column(x, [[part[c, x, z] for c in range(4)] for z in range(8)]) for x in (q, q + 2)]
        pack(q, *pair)
        return 0

    lax.fori_loop(0, 2, outer_pair, 0)
    lax.fori_loop(2, 4, inner_pair, 0)


def kernel_call(kernel, name, given, results, scratch=(), spaces=None, out_spaces=None, limit=48):
    return pl.pallas_call(
        kernel,
        out_shape=results,
        in_specs=spaces or [vmem()] * len(given),
        out_specs=out_spaces or (vmem(),) * len(results),
        scratch_shapes=list(scratch),
        compiler_params=pltpu.CompilerParams(vmem_limit_bytes=limit << 20),
        cost_estimate=pl.CostEstimate(flops=1000, bytes_accessed=1000, transcendentals=0),
        name=name,
    )(*given)


def on_device(density, momentum, column_shift, column_fraction, shear_offset):
    tile = lambda *lead: jax.ShapeDtypeStruct(lead + (8, 128), F32)
    far = pl.BlockSpec(memory_space=pl.ANY)
    moving = [pltpu.VMEM((4, 8, 64, 128), F32), pltpu.SemaphoreType.DMA((4,))]
    (send,) = kernel_call(
        pack_kernel,
        "pack",
        (density, momentum),
        (tile(16, 4, 4),),
        [
            moving[0],
            pltpu.VMEM((4, 16, 4, 8, 128), F32),
            moving[1],
            pltpu.SemaphoreType.DMA((4,)),
        ],
        spaces=[far, far],
        out_spaces=(far,),
        limit=60,
    )
    recv = lax.all_to_all(send, "gy", 0, 0)
    gx, offset = lax.axis_index("gx"), shear_offset[0]
    shifts = lax.dynamic_slice(column_shift, (8 * gx,), (8,))
    leaving = jnp.concatenate(
        [shifts[:2] - jnp.where(gx == 0, offset, 0), shifts[6:] + jnp.where(gx == 7, offset, 0)]
    )
    table = jnp.concatenate([shifts, leaving & 1023, jnp.zeros((116,), jnp.int32)])
    weights = lax.dynamic_slice(column_fraction, (8 * gx,), (8,))
    weights = jnp.broadcast_to(weights[:, None, None], (8, 8, 128))
    rem, x_first, x_second, z_inner, z_outer = kernel_call(
        remap_kernel,
        "remap",
        (table, weights, recv.reshape(2048, 128)),
        (tile(4, 8, 8), tile(4, 2, 8), tile(4, 2, 8), tile(4, 8, 2), tile(4, 8, 2)),
        [
            pltpu.VMEM((4, 8, 8, 8, 128), F32),
            pltpu.SMEM((128,), jnp.int32),
            pltpu.SemaphoreType.DMA,
        ],
        spaces=[far, vmem(), vmem()],
    )
    results = (tile(4, 8, 8),) + (tile(4, 8),) * 4
    rows = rem.reshape(2048, 128)
    *early, x_first, x_second, z_inner, z_outer = kernel_call(
        early_kernel,
        "early",
        (rem, rows, x_first, x_second, z_inner, z_outer),
        results + (tile(4, 2, 8), tile(4, 2, 8), tile(4, 8, 2), tile(4, 8, 2)),
        [pltpu.VMEM((2048, 128), F32)],
    )
    from_first = lax.ppermute(x_first, "gx", [(i, ((i - 1) ^ 1) + 1 & 7) for i in range(8)])
    from_second = lax.ppermute(x_second, "gx", [(i, i ^ 1) for i in range(8)])
    from_inner = lax.ppermute(z_inner, "gy", [(i, i ^ 1) for i in range(16)])
    outer = [(2 * a + g, 2 * b + g) for g in (0, 1) for a, b in zip(PATHS[g][1:-1:2], PATHS[g][2:-1:2])]
    outer.append((2 * PATHS[0][-1], 2 * PATHS[1][-1] + 1))
    from_outer = lax.ppermute(z_outer, ("gy", "gz"), outer + [(b, a) for a, b in outer])

    part, x_minus, x_plus, z_minus, z_plus = kernel_call(
        late_kernel, "late", (rem, rows, *early), results, [pltpu.VMEM((2048, 128), F32)]
    )
    (ends,) = kernel_call(
        radial_kernel, "radial", (part, rem, x_minus, x_plus, from_first, from_second), (tile(4, 4, 8),)
    )
    (send,) = kernel_call(
        vertical_kernel,
        "vertical",
        (part, ends, rem, z_minus, z_plus, from_outer, from_inner),
        (jax.ShapeDtypeStruct((2048, 128), F32),),
    )
    recv = lax.all_to_all(send.reshape(16, 4, 4, 8, 128), "gy", 0, 0)
    return kernel_call(
        unpack_kernel,
        "unpack",
        (recv,),
        (jax.ShapeDtypeStruct(density.shape, F32), jax.ShapeDtypeStruct(momentum.shape, F32)),
        moving,
        out_spaces=(far, far),
    )


def solution(mesh):
    in_specs = (P("gx", "gy", "gz"), P(None, "gx", "gy", "gz"), P(), P(), P())
    out_specs = (P("gx", "gy", "gz"), P(None, "gx", "gy", "gz"))
    return jax.shard_map(
        on_device, mesh=mesh, in_specs=in_specs, out_specs=out_specs, check_vma=False
    )
```

```python
import jax
import jax.numpy as jnp
from jax import lax
from jax.experimental import pallas as pl
from jax.experimental.pallas import tpu as pltpu
from jax.sharding import PartitionSpec as P

def path_of(sign):
    chips = [(y, 0) for y in range(4)] + [(y, 1) for y in (3, 2, 1, 0)]
    return [sign * y % 4 * 4 + xh * 2 + core for y, xh in chips for core in (0, 1)]


PATHS = path_of(1), path_of(-1)
PAIRS = [(0, 6), (1, 7), (2, 4), (3, 5)]
DT = 0.15
F32 = jnp.float32


def vmem():
    return pl.BlockSpec(memory_space=pltpu.VMEM)


def place_of():
    gy, gz = lax.axis_index("gy"), lax.axis_index("gz")
    y = lax.shift_right_logical(gy, 2)
    y = jnp.where(gz == 0, y, -y) & 3
    xh, core = lax.shift_right_logical(gy, 1) & 1, gy & 1
    return 2 * jnp.where(xh == 0, y, 7 - y) + core, core, gz


def owners():
    gz = lax.axis_index("gz")
    return [jnp.where(gz == 0, a, b) for a, b in zip(PATHS[0], PATHS[1][::-1])]


def component_copies(density, momentum, held, sems, outward):
    copies = []
    for c in range(4):
        far, near = density if c == 0 else momentum.at[c - 1], held.at[c]
        source, target = (near, far) if outward else (far, near)
        copies.append(pltpu.make_async_copy(source, target, sems.at[c]))
    return copies


def pack_kernel(density, momentum, send, held, packed, sems, send_sems):
    copies = component_copies(density, momentum, held, sems, False)
    for copy in copies:
        copy.start()
    to = owners()
    leaving = []
    for c in range(4):
        copies[c].wait()
        for q, (a, b) in enumerate(PAIRS):
            turned = jnp.concatenate([held[c, a], held[c, b]], axis=0).T
            for k, device in enumerate(to):
                packed[c, device, q] = turned[8 * k : 8 * k + 8]
        leaving.append(pltpu.make_async_copy(packed.at[c], send.at[:, c], send_sems.at[c]))
        leaving[c].start()
    for copy in leaving:
        copy.wait()


def unpack_kernel(recv, density, momentum, held, sems):
    copies = component_copies(density, momentum, held, sems, True)
    given = owners()
    for c in range(4):
        for q, (a, b) in enumerate(PAIRS):
            turned = jnp.concatenate([recv[device, c, q] for device in given], axis=0).T
            held[c, a] = turned[:64]
            held[c, b] = turned[64:]
        copies[c].start()
    for copy in copies:
        copy.wait()


def lanes():
    return lax.broadcasted_iota(jnp.int32, (8, 128), 1)


def ring_roll(tile, shift, lane):
    far, near = shift // 128, shift % 128
    turned = pltpu.roll(tile, near, 1)
    return jnp.where(lane < near, pltpu.roll(turned, far + 1, 0), pltpu.roll(turned, far, 0))


def ring_next(tile, lane):
    turned = pltpu.roll(tile, 127, 1)
    return jnp.where(lane == 127, pltpu.roll(turned, 7, 0), turned)


def ring_prev(tile, lane):
    turned = pltpu.roll(tile, 1, 1)
    return jnp.where(lane == 0, pltpu.roll(turned, 1, 0), turned)


def remap_kernel(table, weights, recv, rem, x_first, x_second, z_inner, z_outer, mixed, shifts, sem):
    fetch = pltpu.make_async_copy(table, shifts, sem)
    fetch.start()
    lane = lanes()
    _, core, gz = place_of()
    odd = (lax.axis_index("gx") & 1) == 1
    inner_is_high = (core ^ gz) == 0

    def mix(c, _):
        for q, columns in enumerate(PAIRS):
            weight = [weights[x] for x in columns]
            for z in range(8):
                base = (c * 4 + q) * 8 + z
                even = recv[pl.ds(base, 8, stride=256), :]
                odd = recv[pl.ds(base + 128, 8, stride=256), :]
                tiles = (
                    jnp.where(lane < 64, even, pltpu.roll(odd, 64, 1)),
                    jnp.where(lane < 64, pltpu.roll(even, 64, 1), odd),
                )
                for tile, w, x in zip(tiles, weight, columns):
                    mixed[c, x, z] = (1.0 - w) * tile + w * ring_prev(tile, lane)
        return 0

    lax.fori_loop(0, 4, mix, 0)
    fetch.wait()

    def move(c, _):
        leaving = {}
        for x in range(8):
            ends = []
            for z in range(8):
                value = ring_roll(mixed[c, x, z], shifts[x], lane)
                rem[c, x, z] = value
                if z < 2 or z >= 6:
                    ends.append(value)
                if x < 2:
                    leaving[x, z] = ring_roll(mixed[c, x, z], shifts[8 + x], lane)
                if x >= 6:
                    leaving[x, z] = ring_roll(mixed[c, x, z], shifts[4 + x], lane)
            for g in range(2):
                z_inner[c, x, g] = jnp.where(inner_is_high, ends[2 + g], ends[g])
                z_outer[c, x, g] = jnp.where(inner_is_high, ends[g], ends[2 + g])
        for x in range(2):
            for z in range(8):
                x_first[c, x, z] = jnp.where(odd, leaving[6 + x, z], leaving[x, z])
                x_second[c, x, z] = jnp.where(odd, leaving[x, z], leaving[6 + x, z])
        return 0

    lax.fori_loop(0, 4, move, 0)


def minmod(a, b):
    return jnp.maximum(jnp.minimum(a, b), 0.0) + jnp.minimum(jnp.maximum(a, b), 0.0)


def inverse(a):
    first = pl.reciprocal(a, approx=True)
    return first * (2.0 - a * first)


def predict(cell, below, above, k):
    slope = [minmod(below[c], above[c]) for c in range(4)]
    half = [0.5 * s for s in slope]
    minus = [cell[c] - half[c] for c in range(4)]
    plus = [cell[c] + half[c] for c in range(4)]
    v_minus = minus[k] * inverse(minus[0])
    v_plus = plus[k] * inverse(plus[0])
    change = [0.075 * slope[k]]
    for c in range(1, 4):
        term = plus[c] * v_plus - minus[c] * v_minus
        if c == k:
            term = term + slope[0]
        change.append(0.075 * term)
    return [minus[c] - change[c] for c in range(4)], [plus[c] - change[c] for c in range(4)]


def face_flux(left, right, k, v_left, v_right):
    slowest = jnp.minimum(jnp.minimum(v_left, v_right) - 1.0, 0.0)
    fastest = jnp.maximum(jnp.maximum(v_left, v_right) + 1.0, 0.0)
    scale = inverse(fastest - slowest)
    up = fastest * scale
    down = -slowest * scale
    mix = fastest * slowest * scale
    from_left = up * v_left - mix
    from_right = down * v_right + mix
    flux = [left[c] * from_left + right[c] * from_right for c in range(4)]
    flux[k] = flux[k] + (up * left[0] + down * right[0])
    return flux


def along(rem, acc):
    lane = lanes()
    place, _, gz = place_of()
    base = 128 * gz + 8 * jnp.where(gz == 0, place, 15 - place)
    level = base + lax.broadcasted_iota(jnp.int32, (8, 128), 0)
    height = (level.astype(F32) + (0.5 - 128.0)) * (1.0 / 128.0)

    def one(x, _):
        def rows(c, p):
            return pl.ds((c * 8 + x) * 64 + p, 8, stride=8)

        def upward(tiles):
            return [pltpu.roll(t, 1, 1) for t in tiles]

        def downward(tiles):
            return [pltpu.roll(t, 127, 1) for t in tiles]

        def first_from(here, before):
            return [jnp.where(lane == 0, b, h) for h, b in zip(here, before)]

        def last_from(here, after):
            return [jnp.where(lane == 127, b, h) for h, b in zip(here, after)]

        def load(p):
            return [rem[rows(c, p), :] for c in range(4)]

        def differ(p, before):
            cell = load(p)
            turned = upward(cell)
            below = [u - w for u, w in zip(cell, first_from(turned, before))]
            return cell, below, downward(below), turned

        def store(p, flux, before):
            cell = load(p)
            div = [f - w for f, w in zip(flux, before)]
            acc[rows(0, p), :] = cell[0] - DT * div[0]
            acc[rows(1, p), :] = cell[1] - DT * (div[1] - 2.0 * cell[2])
            acc[rows(2, p), :] = cell[2] - DT * (div[2] + 0.5 * cell[1])
            acc[rows(3, p), :] = cell[3] - DT * (div[3] + height * cell[0])

        state = differ(0, upward(load(7)))
        first_down = state[2]
        first_minus = first_flux = minus_before = plus_before = flux_turned = None
        for p in range(9):
            if p < 8:
                cell, below, down, turned = state
                if p < 7:
                    state = differ(p + 1, turned)
                above = last_from(down, state[2] if p < 7 else first_down)
                minus, plus = predict(cell, below, above, 2)
                minus_down = downward(minus)
                if p == 0:
                    first_minus = minus_down
            else:
                minus_down, plus = first_minus, None
            if p > 0:
                right = last_from(minus_before, minus_down)
                flux = face_flux(
                    plus_before,
                    right,
                    2,
                    plus_before[2] * inverse(plus_before[0]),
                    right[2] * inverse(right[0]),
                )
                up = upward(flux)
                if p == 1:
                    first_flux = flux, up
                else:
                    store(p - 1, flux, first_from(up, flux_turned))
                flux_turned = up
            minus_before, plus_before = minus_down, plus
        store(0, first_flux[0], first_from(first_flux[1], flux_turned))
        return 0

    lax.fori_loop(0, 8, one, 0, unroll=2)


def face(left, right, k):
    return face_flux(left, right, k, left[k] * inverse(left[0]), right[k] * inverse(right[0]))


def less(cell, flux):
    return [u - DT * f for u, f in zip(cell, flux)]


def more(cell, flux):
    return [u + DT * f for u, f in zip(cell, flux)]


def difference(upper, lower):
    return [a - b for a, b in zip(upper, lower)]


def march(cells, k):
    fluxes = []
    first_minus = plus_before = None
    below = difference(cells[1], cells[0])
    for i in range(1, 7):
        above = difference(cells[i + 1], cells[i])
        minus, plus = predict(cells[i], below, above, k)
        below = above
        if i == 1:
            first_minus = minus
        else:
            fluxes.append(face(plus_before, minus, k))
        plus_before = plus
    return fluxes, first_minus, plus_before


def low_end(ghosts, cells, minus, k):
    outside, inside = difference(ghosts[1], ghosts[0]), difference(cells[1], cells[0])
    between = difference(cells[0], ghosts[1])
    _, plus_ghost = predict(ghosts[1], outside, between, k)
    minus_cell, plus_cell = predict(cells[0], between, inside, k)
    return face(plus_ghost, minus_cell, k), face(plus_cell, minus, k)


def high_end(ghosts, cells, plus, k):
    outside, inside = difference(ghosts[1], ghosts[0]), difference(cells[1], cells[0])
    between = difference(ghosts[0], cells[1])
    minus_cell, plus_cell = predict(cells[1], inside, between, k)
    minus_ghost, _ = predict(ghosts[0], between, outside, k)
    return face(plus, minus_cell, k), face(plus_cell, minus_ghost, k)


def inside(acc, rem, part, x_minus, x_plus, z_minus, z_plus):
    def line(cells, values, k):
        fluxes, minus, plus = march(cells, k)
        values[1] = less(values[1], fluxes[0])
        for i in range(2, 6):
            values[i] = less(values[i], difference(fluxes[i - 1], fluxes[i - 2]))
        values[6] = more(values[6], fluxes[4])
        return values, minus, plus

    def radial(z, _):
        cells = [[rem[c, x, z] for c in range(4)] for x in range(8)]
        values = [
            [acc[pl.ds(pl.multiple_of(((c * 8 + x) * 8 + z) * 8, 8), 8), :] for c in range(4)]
            for x in range(8)
        ]
        values, minus, plus = line(cells, values, 1)
        for c in range(4):
            for x in range(8):
                part[c, x, z] = values[x][c]
            x_minus[c, z] = minus[c]
            x_plus[c, z] = plus[c]
        return 0

    def vertical(x, _):
        cells = [[rem[c, x, z] for c in range(4)] for z in range(8)]
        values = [[part[c, x, z] for c in range(4)] for z in range(8)]
        values, minus, plus = line(cells, values, 3)
        for c in range(4):
            for z in range(1, 7):
                part[c, x, z] = values[z][c]
            z_minus[c, x] = minus[c]
            z_plus[c, x] = plus[c]
        return 0

    lax.fori_loop(0, 8, radial, 0, unroll=2)
    lax.fori_loop(0, 8, vertical, 0, unroll=2)


def waits_long():
    return lax.axis_index("gx") == 0


def early_kernel(rem, rem_rows, x_first, x_second, z_inner, z_outer, *refs):
    part, x_minus, x_plus, z_minus, z_plus, first_out, second_out, inner_out, outer_out, acc = refs

    @pl.when(waits_long())
    def _():
        along(rem_rows, acc)
        inside(acc, rem, part, x_minus, x_plus, z_minus, z_plus)

    def pass_on(c, _):
        first_out[c] = x_first[c]
        second_out[c] = x_second[c]
        inner_out[c] = z_inner[c]
        outer_out[c] = z_outer[c]
        return 0

    lax.fori_loop(0, 4, pass_on, 0)


def late_kernel(rem, rem_rows, *refs):
    done, (*results, acc) = refs[:5], refs[5:]
    early = waits_long()

    @pl.when(early)
    def _():
        def pass_on(c, _):
            for given, result in zip(done, results):
                result[c] = given[c]
            return 0

        lax.fori_loop(0, 4, pass_on, 0)

    @pl.when(jnp.logical_not(early))
    def _():
        along(rem_rows, acc)
        inside(acc, rem, *results)


def radial_kernel(part, rem, x_minus, x_plus, from_first, from_second, ends):
    odd = (lax.axis_index("gx") & 1) == 1

    def one(z, _):
        def at(ref, x):
            return [ref[c, x, z] for c in range(4)]

        def ghosts(low):
            pairs = [zip(at(from_first, x), at(from_second, x)) for x in range(2)]
            return [[jnp.where(odd == low, b, a) for a, b in pair] for pair in pairs]

        below, above = low_end(
            ghosts(True),
            [at(rem, 0), at(rem, 1)],
            [x_minus[c, z] for c in range(4)],
            1,
        )
        values = [less(at(part, 0), difference(above, below)), more(at(part, 1), above)]
        below, above = high_end(
            ghosts(False),
            [at(rem, 6), at(rem, 7)],
            [x_plus[c, z] for c in range(4)],
            1,
        )
        values += [less(at(part, 6), below), less(at(part, 7), difference(above, below))]
        for i, value in enumerate(values):
            for c in range(4):
                ends[c, i, z] = value[c]
        return 0

    lax.fori_loop(0, 8, one, 0, unroll=2)


def vertical_kernel(part, ends, rem, z_minus, z_plus, from_outer, from_inner, send):
    lane = lanes()
    place, core, gz = place_of()
    inner_is_high = (core ^ gz) == 0
    at_end = place == 0

    def column(x, values):
        def at(z):
            return [rem[c, x, z] for c in range(4)]

        cells = {z: at(z) for z in (0, 1, 6, 7)}
        low, high = [], []
        for g in range(2):
            near = [from_inner[c, x, g] for c in range(4)]
            far = [from_outer[c, x, g] for c in range(4)]
            end = [jnp.where(inner_is_high, a, b) for a, b in zip(cells[0], cells[7])]
            far = [jnp.where(at_end, a, b) for a, b in zip(end, far)]
            low.append([jnp.where(inner_is_high, a, b) for a, b in zip(far, near)])
            high.append([jnp.where(inner_is_high, a, b) for a, b in zip(near, far)])
        below, above = low_end(low, [cells[0], cells[1]], [z_minus[c, x] for c in range(4)], 3)
        values[0], values[1] = less(values[0], difference(above, below)), more(values[1], above)
        below, above = high_end(high, [cells[6], cells[7]], [z_plus[c, x] for c in range(4)], 3)
        values[6], values[7] = less(values[6], below), less(values[7], difference(above, below))
        return values

    def pack(q, first, second):
        for z in range(8):
            for c in range(4):
                base = (c * 4 + q) * 8 + z
                a, b = first[z][c], second[z][c]
                send[pl.ds(base, 8, stride=256), :] = jnp.where(lane < 64, a, pltpu.roll(b, 64, 1))
                send[pl.ds(base + 128, 8, stride=256), :] = jnp.where(lane < 64, pltpu.roll(a, 64, 1), b)

    def outer_pair(q, _):
        pair = [
            column(x, [[ends[c, i, z] for c in range(4)] for z in range(8)])
            for x, i in ((q, q), (q + 6, q + 2))
        ]
        pack(q, *pair)
        return 0

    def inner_pair(q, _):
        pair = [column(x, [[part[c, x, z] for c in range(4)] for z in range(8)]) for x in (q, q + 2)]
        pack(q, *pair)
        return 0

    lax.fori_loop(0, 2, outer_pair, 0)
    lax.fori_loop(2, 4, inner_pair, 0)


def kernel_call(kernel, name, given, results, scratch=(), spaces=None, out_spaces=None, limit=48):
    return pl.pallas_call(
        kernel,
        out_shape=results,
        in_specs=spaces or [vmem()] * len(given),
        out_specs=out_spaces or (vmem(),) * len(results),
        scratch_shapes=list(scratch),
        compiler_params=pltpu.CompilerParams(vmem_limit_bytes=limit << 20),
        cost_estimate=pl.CostEstimate(flops=1000, bytes_accessed=1000, transcendentals=0),
        name=name,
    )(*given)


def on_device(density, momentum, column_shift, column_fraction, shear_offset):
    tile = lambda *lead: jax.ShapeDtypeStruct(lead + (8, 128), F32)
    far = pl.BlockSpec(memory_space=pl.ANY)
    moving = [pltpu.VMEM((4, 8, 64, 128), F32), pltpu.SemaphoreType.DMA((4,))]
    (send,) = kernel_call(
        pack_kernel,
        "pack",
        (density, momentum),
        (tile(16, 4, 4),),
        [
            moving[0],
            pltpu.VMEM((4, 16, 4, 8, 128), F32),
            moving[1],
            pltpu.SemaphoreType.DMA((4,)),
        ],
        spaces=[far, far],
        out_spaces=(far,),
        limit=60,
    )
    recv = lax.all_to_all(send, "gy", 0, 0)
    gx, offset = lax.axis_index("gx"), shear_offset[0]
    shifts = lax.dynamic_slice(column_shift, (8 * gx,), (8,))
    leaving = jnp.concatenate(
        [shifts[:2] - jnp.where(gx == 0, offset, 0), shifts[6:] + jnp.where(gx == 7, offset, 0)]
    )
    table = jnp.concatenate([shifts, leaving & 1023, jnp.zeros((116,), jnp.int32)])
    weights = lax.dynamic_slice(column_fraction, (8 * gx,), (8,))
    weights = jnp.broadcast_to(weights[:, None, None], (8, 8, 128))
    rem, x_first, x_second, z_inner, z_outer = kernel_call(
        remap_kernel,
        "remap",
        (table, weights, recv.reshape(2048, 128)),
        (tile(4, 8, 8), tile(4, 2, 8), tile(4, 2, 8), tile(4, 8, 2), tile(4, 8, 2)),
        [
            pltpu.VMEM((4, 8, 8, 8, 128), F32),
            pltpu.SMEM((128,), jnp.int32),
            pltpu.SemaphoreType.DMA,
        ],
        spaces=[far, vmem(), vmem()],
    )
    results = (tile(4, 8, 8),) + (tile(4, 8),) * 4
    rows = rem.reshape(2048, 128)
    *early, x_first, x_second, z_inner, z_outer = kernel_call(
        early_kernel,
        "early",
        (rem, rows, x_first, x_second, z_inner, z_outer),
        results + (tile(4, 2, 8), tile(4, 2, 8), tile(4, 8, 2), tile(4, 8, 2)),
        [pltpu.VMEM((2048, 128), F32)],
    )
    from_first = lax.ppermute(x_first, "gx", [(i, ((i - 1) ^ 1) + 1 & 7) for i in range(8)])
    from_second = lax.ppermute(x_second, "gx", [(i, i ^ 1) for i in range(8)])
    from_inner = lax.ppermute(z_inner, "gy", [(i, i ^ 1) for i in range(16)])
    outer = [(2 * a + g, 2 * b + g) for g in (0, 1) for a, b in zip(PATHS[g][1:-1:2], PATHS[g][2:-1:2])]
    outer.append((2 * PATHS[0][-1], 2 * PATHS[1][-1] + 1))
    from_outer = lax.ppermute(z_outer, ("gy", "gz"), outer + [(b, a) for a, b in outer])

    part, x_minus, x_plus, z_minus, z_plus = kernel_call(
        late_kernel, "late", (rem, rows, *early), results, [pltpu.VMEM((2048, 128), F32)]
    )
    (ends,) = kernel_call(
        radial_kernel, "radial", (part, rem, x_minus, x_plus, from_first, from_second), (tile(4, 4, 8),)
    )
    (send,) = kernel_call(
        vertical_kernel,
        "vertical",
        (part, ends, rem, z_minus, z_plus, from_outer, from_inner),
        (jax.ShapeDtypeStruct((2048, 128), F32),),
    )
    recv = lax.all_to_all(send.reshape(16, 4, 4, 8, 128), "gy", 0, 0)
    return kernel_call(
        unpack_kernel,
        "unpack",
        (recv,),
        (jax.ShapeDtypeStruct(density.shape, F32), jax.ShapeDtypeStruct(momentum.shape, F32)),
        moving,
        out_spaces=(far, far),
    )


def solution(mesh):
    in_specs = (P("gx", "gy", "gz"), P(None, "gx", "gy", "gz"), P(), P(), P())
    out_specs = (P("gx", "gy", "gz"), P(None, "gx", "gy", "gz"))
    return jax.shard_map(
        on_device, mesh=mesh, in_specs=in_specs, out_specs=out_specs, check_vma=False
    )
```
